1024 devices in a mesh: dp: 64 (over y_lo, z), expert: 16 (over x, y_hi, core).
Axes of the slice: x: 4, y: 4 (y_hi: 2, y_lo: 2; y = y_hi * 2 + y_lo), z: 32, core: 2. Of those that a mesh axis runs over, the one named last changes fastest.
Arguments:
- tokens: bfloat16 [131072, 2048], P(('dp', 'expert')), may hold values from -6 to 6
- cotangent: bfloat16 [131072, 2048], P(('dp', 'expert')), may hold values from -6 to 6
- expert_ids: int32 [131072, 2], P(('dp', 'expert')), may hold values from 0 to 15, all different within a row; in each aligned block of 128 rows (0 to 127, 128 to 255, ...) at most 18 rows name the same one
- gate_values: bfloat16 [131072, 2], P(('dp', 'expert')), may hold values from 0.099609375 to 1
- gate_weights: bfloat16 [16, 2048, 512], P('expert'), may hold values from -0.125 to 0.125
- up_weights: bfloat16 [16, 2048, 512], P('expert'), may hold values from -0.125 to 0.125
- down_weights: bfloat16 [16, 512, 2048], P('expert'), may hold values from -0.25 to 0.25
Outputs:
- token_grads: bfloat16 [131072, 2048], P(('dp', 'expert'))
- down_grads: float32 [16, 512, 2048], P('expert', 'dp')
The draws below stay inside these ranges and needn't reach their ends.
Inputs may be any that keep to these rules, and one draw needn't show every extreme that they name: `expert_ids`: within the rows of one device, each expert is named by at most 18 slots, and by exactly 18 slots in the rows of some device.
All inputs are finite; a program needn't handle non-finite values.
Results may differ from the reference program's by a relative error of at most 0.0065.
Values may be sent and summed in bfloat16 or wider, within the bound.
A program may use at most 64 MiB of HBM per device.

```python
import math
import jax
import jax.numpy as jnp
import numpy as np
from jax import lax

D = 2048
F = 512
TOP = 2
TOK_DEV = 128
EXPERTS = 16
CAP = 18
TOKENS = 131072


def steps_of(stream_key, dims, split, smallest, high):
    def one(axis_at, parts):
        draws = jax.random.uniform(jax.random.fold_in(jax.random.fold_in(stream_key, 6), axis_at), (parts,), jnp.float32, smallest / len(split), high / len(split))
        return jnp.repeat(jnp.exp(draws), dims[axis_at] // parts).reshape((-1,) + (1,) * (len(dims) - axis_at - 1))

    gain = one(*split[0])
    for cut in split[1:]:
        gain = gain * one(*cut)
    return gain


def assign_block(rng, own, number, rows, number_of, top, limit, skew):
    sequence = jax.random.permutation(rng, number_of)
    packed, usual = portions_of(number_of, rows * top, limit, skew, True), portions_of(number_of, rows * top, limit, skew, False)
    places = jnp.arange(number_of)

    def named(tallies, rotation):
        used = int((tallies > 0).sum())
        fixed = max(1, used // 4)
        shifted = fixed + (places - fixed + rotation * (used - fixed)) % max(1, number_of - fixed)
        return jnp.zeros((number_of,), jnp.int32).at[sequence[jnp.where(places < fixed, places, shifted)]].set(jnp.asarray(tallies, jnp.int32))

    tallies = jnp.where(number % 4 == 0, named(packed, number // 4), named(usual, number - number // 4 - 1))
    mixed = jax.random.permutation(jax.random.fold_in(own, 3), number_of)
    source_of, sink = mixed[0:number_of // 2 * 2:2], mixed[1:number_of // 2 * 2:2]
    room = jnp.minimum(tallies[source_of] - 1, limit - tallies[sink]) // 2
    room = jnp.where((source_of == sequence[0]) | (sink == sequence[0]) | (tallies[sink] == 0), 0, jnp.maximum(room, 0))
    shifted = jax.random.randint(jax.random.fold_in(own, 4), (number_of // 2,), 0, 1 << 20) % (room + 1)
    tallies = tallies.at[source_of].add(-shifted).at[sink].add(shifted)
    items = jnp.searchsorted(jnp.cumsum(tallies), jnp.arange(rows * top), side="right").astype(jnp.int32)
    listing = items.reshape(top, rows).T
    listing = listing[jax.random.permutation(jax.random.fold_in(own, 1), rows)]
    rotation = jax.random.randint(jax.random.fold_in(own, 2), (rows, 1), 0, top)
    return jnp.take_along_axis(listing, (jnp.arange(top)[None, :] + rotation) % top, axis=1)


def portions_of(amount, total, reach, lean, full):
    weights = [(1 << 20) // math.isqrt(standing ** lean) + 1 for standing in range(1, amount + 1)]
    largest = reach if full else min(reach, max(-(-total // amount), total * weights[0] // sum(weights)))
    least = 1 if total - largest >= amount - 1 else 0
    counts, surplus = [largest] + [least] * (amount - 1), total - largest - least * (amount - 1)
    while surplus > 0:
        free = [i for i in range(1, amount) if counts[i] < largest] or [i for i in range(1, amount) if counts[i] < reach]
        mass, remaining = sum([weights[i] for i in free]), surplus
        for i in free:
            more = min(reach - counts[i], max(1, remaining * weights[i] // mass), surplus)
            counts[i] = counts[i] + more
            surplus = surplus - more
    return np.array(counts)


def normal_values(stream_key, extent, width, limit, shards=(), kind=jnp.bfloat16):
    values = width * jax.random.normal(stream_key, extent, jnp.float32)
    if shards:
        values = values * steps_of(stream_key, extent, shards, -0.22, 0.18)
    return jnp.clip(values, -limit, limit).astype(kind)


def setup_inputs(seed: int = 0) -> dict:
    splits = jax.random.split(jax.random.key(seed), 8)
    tokens = normal_values(splits[0], (TOKENS, D), 1.0, 6.0, ((0, 1024),))
    cotangent = normal_values(splits[1], (TOKENS, D), 1.0, 6.0, ((0, 1024),))
    expert_ids_keys = jax.random.split(jax.random.fold_in(splits[2], 1), TOKENS // TOK_DEV)
    expert_ids_turns = jax.random.permutation(jax.random.fold_in(splits[2], 3), TOKENS // TOK_DEV)
    expert_ids = jax.vmap(lambda own, number: assign_block(jax.random.fold_in(splits[2], 2), own, number, TOK_DEV, EXPERTS, TOP, CAP, 2))(expert_ids_keys, expert_ids_turns).reshape((TOKENS, TOP))
    gate_values = jnp.clip(0.099609375 + 0.9003906 * jax.random.uniform(splits[3], (TOKENS, TOP), jnp.float32) ** steps_of(splits[3], (TOKENS, TOP), ((0, 1024),), -0.2, 0.2), 0.099609375, 1.0).astype(jnp.bfloat16)
    gate_weights = normal_values(splits[4], (EXPERTS, D, F), D ** -0.5, 0.125, ((0, 16),))
    up_weights = normal_values(splits[5], (EXPERTS, D, F), D ** -0.5, 0.125, ((0, 16),))
    down_weights = normal_values(splits[6], (EXPERTS, F, D), F ** -0.5, 0.25, ((0, 16),))
    return dict(tokens=tokens, cotangent=cotangent, expert_ids=expert_ids, gate_values=gate_values, gate_weights=gate_weights, up_weights=up_weights, down_weights=down_weights)


def expert_pass(rows_x, rows_dy, rows_gates, w_gate, w_up, w_down):
    pre_gate = jnp.dot(rows_x, w_gate, preferred_element_type=jnp.float32)
    pre_up = jnp.dot(rows_x, w_up, preferred_element_type=jnp.float32)
    sigmoid_of = jax.nn.sigmoid(pre_gate)
    activated = pre_gate * sigmoid_of
    hidden = (activated * pre_up).astype(jnp.bfloat16)
    scaled = (rows_gates[:, None].astype(jnp.float32) * rows_dy.astype(jnp.float32)).astype(jnp.bfloat16)
    down_grad = lax.dot_general(hidden, scaled, (((0,), (0,)), ((), ())), preferred_element_type=jnp.float32)
    contract_cols = (((1,), (1,)), ((), ()))
    hidden_back = lax.dot_general(scaled, w_down, contract_cols, preferred_element_type=jnp.float32)
    gate_back = (hidden_back * pre_up * sigmoid_of * (1.0 + pre_gate * (1.0 - sigmoid_of))).astype(jnp.bfloat16)
    up_back = (hidden_back * activated).astype(jnp.bfloat16)
    row_grads = lax.dot_general(gate_back, w_gate, contract_cols, preferred_element_type=jnp.float32)
    row_grads = row_grads + lax.dot_general(up_back, w_up, contract_cols, preferred_element_type=jnp.float32)
    return row_grads.astype(jnp.bfloat16), down_grad


def reference(tokens, cotangent, expert_ids, gate_values, gate_weights, up_weights, down_weights):
    blocks = TOKENS // TOK_DEV
    per_block = TOK_DEV * TOP
    slot_total = TOKENS * TOP
    ids_blocks = expert_ids.reshape(blocks, per_block)
    columns = jnp.arange(EXPERTS).astype(jnp.int32)
    one_hot = (ids_blocks[:, :, None] == columns[None, None, :]).astype(jnp.int32)
    earlier = jnp.cumsum(one_hot, axis=1) - one_hot
    position = jnp.sum(one_hot * earlier, axis=2).astype(jnp.int32)
    block_index = jnp.arange(blocks).astype(jnp.int32)[:, None]
    target = ids_blocks * (blocks * CAP) + block_index * CAP + position
    slot_ids = jnp.arange(slot_total).astype(jnp.int32)
    table = jnp.full((EXPERTS * blocks * CAP,), slot_total, jnp.int32)
    table = table.at[target.reshape(-1).astype(jnp.int32)].set(slot_ids).reshape(EXPERTS, blocks * CAP)
    flat_gates = gate_values.reshape(slot_total)

    def per_expert(running, inputs):
        slot_list, w_gate, w_up, w_down = inputs
        token_rows = (slot_list // TOP).astype(jnp.int32)
        rows_x = jnp.take(tokens, token_rows, axis=0, mode="fill", fill_value=0)
        rows_dy = jnp.take(cotangent, token_rows, axis=0, mode="fill", fill_value=0)
        rows_gates = jnp.take(flat_gates, slot_list, axis=0, mode="fill", fill_value=0)
        row_grads, down_grad = expert_pass(rows_x, rows_dy, rows_gates, w_gate, w_up, w_down)
        running = running.at[token_rows].add(row_grads.astype(jnp.float32), mode="drop")
        return running, down_grad

    accumulated, down_grads = lax.scan(per_expert, jnp.zeros((TOKENS, D), jnp.float32), (table, gate_weights, up_weights, down_weights))
    return accumulated.astype(jnp.bfloat16), down_grads
```

```python
import functools

import jax
import jax.numpy as jnp
from jax import lax
from jax.experimental import pallas as pl
from jax.experimental.pallas import tpu as pltpu
from jax.sharding import PartitionSpec as P

MESH = pl.DeviceIdType.MESH
F32, BF16 = jnp.float32, jnp.bfloat16
NT = (((1,), (1,)), ((), ()))
OFFSETS = (
    (2, 1, 0), (1, 0, 0), (3, 1, 0), (2, 0, 1), (1, 1, 1), (3, 0, 0), (0, 1, 0), (2, 0, 0),
    (1, 0, 1), (3, 1, 1), (2, 1, 1), (1, 1, 0), (3, 0, 1), (0, 1, 1), (0, 0, 1),
)


def nn(a, b):
    return jnp.dot(a, b, preferred_element_type=F32)


def nt(a, b):
    return lax.dot_general(a, b, NT, preferred_element_type=F32)


def kernel(
    nz, nx,
    tok, cot, ids, gates, wg_hbm, wu_hbm, wd_hbm,
    out_tok, out_down,
    wg, wu, wd, xs, xr, sd, sr, rd, rr, sel, selt, perm, hid, hidt, act, mix, hb, gb, ub,
    part, psend, precv, rsend, rrecv, fin, ybuf,
    wsem, lsem, ssem, rsem, psem, prsem, gsem, grsem, ysem,
):
    toks, width = tok.shape
    half = width // 2
    lanes = 128
    cols = half // lanes
    experts = nx * 4
    main, more = 16 * experts, 2 * experts
    rows = main + more
    hidden = wg.shape[1]
    dp, me = lax.axis_index("dp"), lax.axis_index("expert")
    yl, z = dp // nz, dp % nz
    x, yh, c = me // 4, (me // 2) % 2, me % 2

    def at(z2):
        return (yl * nz + z2 % nz, me)

    peers = []
    for dx, dy, dc in OFFSETS:
        if dx < nx:
            x2, yh2, c2, yl2 = (x + dx) % nx, (yh + dy) % 2, (c + dc) % 2, (yl + dy) % 2
            e2 = x2 * 4 + yh2 * 2 + c2
            peers.append(((yl2 * nz + z, e2), e2))
    odd = z % 2
    pairs = ((z + 1 - 2 * odd), (z + nz - 1 + 2 * odd) % nz)
    up, down = at(z + 2), at(z + nz - 2)
    across = ((1 - yl) * nz + z, me)

    barrier = pltpu.get_barrier_semaphore()
    greet = [p[0] for p in peers] + [at(p) for p in pairs] + [up, down, across]
    for d in greet:
        pl.semaphore_signal(barrier, inc=1, device_id=d, device_id_type=MESH)

    loads = [
        pltpu.make_async_copy(a, b, wsem.at[i])
        for i, (a, b) in enumerate(((wg_hbm, wg), (wu_hbm, wu), (wd_hbm, wd)))
    ]
    for load in loads:
        load.start()

    def iota(shape, dim):
        return lax.broadcasted_iota(jnp.int32, shape, dim)

    eye = iota((toks, toks), 0) == iota((toks, toks), 1)
    before = (iota((toks, toks), 0) < iota((toks, toks), 1)).astype(F32).astype(BF16)
    idv = ids[...].astype(F32)
    gtv = gates[...].astype(F32)

    def as_row(v):
        return jnp.sum(jnp.where(eye, v, 0.0), axis=0, keepdims=True)

    id_rows = [as_row(idv[:, k : k + 1]) for k in (0, 1)]
    gate_rows = [as_row(gtv[:, k : k + 1]) for k in (0, 1)]
    named = [(iota((experts, toks), 0).astype(F32) == r).astype(F32) for r in id_rows]
    earlier = nn((named[0] + named[1]).astype(BF16), before)
    slot = iota((rows, toks), 0).astype(F32)
    picks = []
    for k in (0, 1):
        pos = jnp.sum(named[k] * earlier, axis=0, keepdims=True)
        target = jnp.where(pos < 16.0, id_rows[k] * 16.0 + pos, main + id_rows[k] * 2.0 + (pos - 16.0))
        picks.append((slot == target).astype(F32))
    sel[...] = (picks[0] + picks[1]).astype(BF16)
    slot_gates = jnp.sum(picks[0] * gate_rows[0] + picks[1] * gate_rows[1], axis=1, keepdims=True)
    r0, r1 = iota((main, main), 0), iota((main, main), 1)
    perm[...] = (r1 == (r0 % cols) * more + r0 // cols).astype(F32).astype(BF16)

    def pack(buf, h):
        tall = jnp.concatenate(
            [buf[h, main:rows, j * lanes : (j + 1) * lanes] for j in range(cols)], axis=0
        )
        buf[h, 0:main, half : half + lanes] = nn(perm[...], tall).astype(BF16)

    def unpack(buf, h):
        tall = lax.dot_general(
            perm[...], buf[h, 0:main, half : half + lanes], (((0,), (0,)), ((), ())),
            preferred_element_type=F32,
        ).astype(BF16)
        for j in range(cols):
            buf[h, main:rows, j * lanes : (j + 1) * lanes] = tall[j * more : (j + 1) * more]

    def gather(src, buf, h, scale):
        def tile(t, carry):
            lo = pl.multiple_of(t * 256, 256)
            v = nn(sel[...], src[:, pl.ds(pl.multiple_of(h * half + lo, 256), 256)])
            if scale is not None:
                v = v * scale
            buf[h, 0:rows, pl.ds(lo, 256)] = v.astype(BF16)
            return carry

        lax.fori_loop(0, half // 256, tile, 0)
        pack(buf, h)

    def swap(unit, src, dst, h):
        mine = pl.ds(pl.multiple_of(me * 16, 16), 16)
        copies = [
            pltpu.make_async_remote_copy(
                src_ref=src.at[h, pl.ds(pl.multiple_of(e2 * 16, 16), 16)],
                dst_ref=dst.at[h, mine],
                send_sem=ssem.at[unit, i], recv_sem=rsem.at[unit, i],
                device_id=dev, device_id_type=MESH,
            )
            for i, (dev, e2) in enumerate(peers)
        ]
        own = pltpu.make_async_copy(src.at[h, mine], dst.at[h, mine], lsem.at[unit])
        return copies, own

    swaps = [
        swap(0, xs, xr, 0), swap(1, xs, xr, 1), swap(2, sd, sr, 0), swap(3, sd, sr, 1),
        swap(4, rd, rr, 0), swap(5, rd, rr, 1),
    ]

    def send(unit):
        copies, own = swaps[unit]
        for copy in copies:
            copy.start()
        own.start()

    def arrive(unit):
        copies, own = swaps[unit]
        for copy in copies:
            copy.wait_recv()
        own.wait()

    gather(tok, xs, 0, None)
    pl.semaphore_wait(barrier, len(greet))
    send(0)
    gather(tok, xs, 1, None)
    send(1)
    gather(cot, sd, 0, slot_gates)
    send(2)
    gather(cot, sd, 1, slot_gates)
    send(3)

    selt[...] = nt(eye.astype(F32).astype(BF16), sel[...]).astype(BF16)
    loads[0].wait()
    loads[1].wait()
    arrive(0)
    arrive(1)
    unpack(xr, 0)
    unpack(xr, 1)

    tile_f = min(256, hidden)

    def first(t, carry):
        f = pl.ds(pl.multiple_of(t * tile_f, tile_f), tile_f)
        gate = nn(xr[0, 0:rows, 0:half], wg[0:half, f]) + nn(xr[1, 0:rows, 0:half], wg[half:width, f])
        upv = nn(xr[0, 0:rows, 0:half], wu[0:half, f]) + nn(xr[1, 0:rows, 0:half], wu[half:width, f])
        s = jax.nn.sigmoid(gate)
        a = gate * s
        hid[:, f] = (a * upv).astype(BF16)
        act[:, f] = a
        mix[:, f] = upv * s * (1.0 + gate * (1.0 - s))
        return carry

    lax.fori_loop(0, hidden // tile_f, first, 0)

    def turn(t, carry):
        lo = pl.multiple_of(t * tile_f, tile_f)
        to = lo + iota((tile_f, hidden), 0)
        par, rest = to // (hidden // 2), to % (hidden // 2)
        zz, low = (rest // 16) * 2 + par, rest % 16
        source = ((low // 8) * nz + zz) * 8 + low % 8
        move = (iota((tile_f, hidden), 1) == source).astype(F32).astype(BF16)
        hidt[pl.ds(lo, tile_f), :] = nt(move, hid[...]).astype(BF16)
        return carry

    lax.fori_loop(0, hidden // tile_f, turn, 0)
    loads[2].wait()

    nodes = nz // 2
    a_mine = z // 2
    steps_up, steps_down = nodes // 2, nodes // 2 - 1

    def chunk(par, a):
        return pl.ds(pl.multiple_of(par * (hidden // 2) + (a % nodes) * 16, 16), 16)

    def order(a):
        found = []
        for k in range(steps_up):
            found.append((a + nodes // 2 - k, "up", k))
            if k < steps_down:
                found.append((a + nodes - steps_down + k, "down", k))
        return found + [(a, "own", 0)]

    def pair_copies(h):
        partner = pairs[h]
        copies = []
        for j, (a, _, _) in enumerate(order(partner // 2)):
            slot_j = pl.ds(j * 16, 16)
            copies.append(
                pltpu.make_async_remote_copy(
                    src_ref=psend.at[h, slot_j], dst_ref=precv.at[h, slot_j],
                    send_sem=psem.at[h, j], recv_sem=prsem.at[h, j],
                    device_id=at(partner), device_id_type=MESH,
                )
            )
        return copies

    pair = [pair_copies(0), pair_copies(1)]
    mine = {(way, k): (j, a) for j, (a, way, k) in enumerate(order(a_mine))}

    def products(h):
        def tile(t, carry):
            lo = pl.ds(pl.multiple_of(t * 256, 256), 256)
            part[h, :, lo] = nn(hidt[...], sr[h, 0:rows, lo])
            return carry

        lax.fori_loop(0, half // 256, tile, 0)
        for j, (a, _, _) in enumerate(order(pairs[h] // 2)):
            psend[h, j * 16 : (j + 1) * 16] = part[h, chunk(1 - odd, a), :].astype(BF16)
            pair[h][j].start()

        def back(t, carry):
            f = pl.ds(pl.multiple_of(t * tile_f, tile_f), tile_f)
            v = nt(sr[h, 0:rows, 0:half], wd[f, h * half : (h + 1) * half])
            hb[:, f] = v if h == 0 else hb[:, f] + v
            return carry

        lax.fori_loop(0, hidden // tile_f, back, 0)

    def ring_copy(h, way, k):
        d = 0 if way == "up" else 1
        span = pl.ds(k * 16, 16)
        return pltpu.make_async_remote_copy(
            src_ref=rsend.at[d, h, span], dst_ref=rrecv.at[d, h, span],
            send_sem=gsem.at[d, h, k], recv_sem=grsem.at[d, h, k],
            device_id=up if way == "up" else down, device_id_type=MESH,
        )

    def own_sum(h, way, k):
        j, a = mine[way, k]
        pair[h][j].wait_recv()
        return part[h, chunk(odd, a), :] + precv[h, j * 16 : (j + 1) * 16].astype(F32)

    def ring_step(k):
        for h in (0, 1):
            for d, (way, steps) in enumerate((("up", steps_up), ("down", steps_down))):
                if k < steps:
                    v = own_sum(h, way, k)
                    if k > 0:
                        ring_copy(h, way, k - 1).wait_recv()
                        v = v + rrecv[d, h, (k - 1) * 16 : k * 16].astype(F32)
                    rsend[d, h, k * 16 : (k + 1) * 16] = v.astype(BF16)
                    ring_copy(h, way, k).start()

    arrive(2)
    unpack(sr, 0)
    products(0)
    arrive(3)
    unpack(sr, 1)
    products(1)

    gb[...] = (hb[...] * mix[...]).astype(BF16)
    ub[...] = (hb[...] * act[...]).astype(BF16)

    def row_grads(h):
        def tile(t, carry):
            lo = pl.multiple_of(t * 256, 256)
            w = pl.ds(pl.multiple_of(h * half + lo, 256), 256)
            rd[h, 0:rows, pl.ds(lo, 256)] = (nt(gb[...], wg[w, :]) + nt(ub[...], wu[w, :])).astype(BF16)
            return carry

        lax.fori_loop(0, half // 256, tile, 0)
        pack(rd, h)

    def combine(h):
        unpack(rr, h)

        def tile(t, carry):
            lo = pl.multiple_of(t * 256, 256)
            w = pl.ds(pl.multiple_of(h * half + lo, 256), 256)
            out_tok[:, w] = nn(selt[...], rr[h, 0:rows, pl.ds(lo, 256)]).astype(BF16)
            return carry

        lax.fori_loop(0, half // 256, tile, 0)

    row_grads(0)
    send(4)
    ring_step(0)
    row_grads(1)
    send(5)
    for k in range(1, steps_up):
        ring_step(k)

    for h in (0, 1):
        v = own_sum(h, "own", 0)
        for d, (way, steps) in enumerate((("up", steps_up), ("down", steps_down))):
            if steps > 0:
                ring_copy(h, way, steps - 1).wait_recv()
                v = v + rrecv[d, h, (steps - 1) * 16 : steps * 16].astype(F32)
        fin[:, h * half : (h + 1) * half] = v
    last = pltpu.make_async_remote_copy(
        src_ref=fin.at[pl.ds(pl.multiple_of((1 - yl) * 8, 8), 8)], dst_ref=ybuf,
        send_sem=ysem.at[0], recv_sem=ysem.at[1], device_id=across, device_id_type=MESH,
    )
    last.start()
    for h in (0, 1):
        arrive(4 + h)
        combine(h)
    last.wait_recv()
    out_down[...] = fin[pl.ds(pl.multiple_of(yl * 8, 8), 8), :] + ybuf[...]

    last.wait_send()
    for copies, _ in swaps:
        for copy in copies:
            copy.wait_send()
    for h in (0, 1):
        for copy in pair[h]:
            copy.wait_send()
        for way, steps in (("up", steps_up), ("down", steps_down)):
            for k in range(steps):
                ring_copy(h, way, k).wait_send()


def solution(mesh):
    nz, experts = mesh.shape["dp"] // 2, mesh.shape["expert"]

    def body(tokens, cotangent, expert_ids, gate_values, gate_weights, up_weights, down_weights):
        toks, width = tokens.shape
        hidden = gate_weights.shape[2]
        half, rows, main = width // 2, 18 * experts, 16 * experts
        n = experts - 1
        nodes = nz // 2
        vmem = pl.BlockSpec(memory_space=pltpu.VMEM)
        hbm = pl.BlockSpec(memory_space=pl.ANY)
        block = pltpu.VMEM((2, rows, half + 128), BF16)
        dma = pltpu.SemaphoreType.DMA
        flops = 2 * rows * width * hidden * 6
        out_tok, out_down = pl.pallas_call(
            functools.partial(kernel, nz, experts // 4),
            out_shape=(
                jax.ShapeDtypeStruct((toks, width), BF16),
                jax.ShapeDtypeStruct((8, width), F32),
            ),
            in_specs=[vmem] * 4 + [hbm] * 3,
            out_specs=(vmem, vmem),
            scratch_shapes=[
                pltpu.VMEM((width, hidden), BF16), pltpu.VMEM((width, hidden), BF16), pltpu.VMEM((hidden, width), BF16),
                block, block, block, block, block, block,
                pltpu.VMEM((rows, toks), BF16), pltpu.VMEM((toks, rows), BF16), pltpu.VMEM((main, main), BF16),
                pltpu.VMEM((rows, hidden), BF16), pltpu.VMEM((hidden, rows), BF16),
                pltpu.VMEM((rows, hidden), F32), pltpu.VMEM((rows, hidden), F32), pltpu.VMEM((rows, hidden), F32),
                pltpu.VMEM((rows, hidden), BF16), pltpu.VMEM((rows, hidden), BF16),
                pltpu.VMEM((2, hidden, half), F32),
                pltpu.VMEM((2, nodes * 16, half), BF16), pltpu.VMEM((2, nodes * 16, half), BF16),
                pltpu.VMEM((2, 2, nodes // 2 * 16, half), BF16), pltpu.VMEM((2, 2, nodes // 2 * 16, half), BF16),
                pltpu.VMEM((16, width), F32), pltpu.VMEM((8, width), F32),
                dma((3,)), dma((6,)), dma((6, n)), dma((6, n)),
                dma((2, nodes)), dma((2, nodes)), dma((2, 2, nodes // 2)), dma((2, 2, nodes // 2)), dma((2,)),
            ],
            compiler_params=pltpu.CompilerParams(
                collective_id=0, has_side_effects=True, vmem_limit_bytes=52 * 2**20
            ),
            cost_estimate=pl.CostEstimate(flops=flops, bytes_accessed=8 * 2**20, transcendentals=rows * hidden),
        )(tokens, cotangent, expert_ids, gate_values, gate_weights[0], up_weights[0], down_weights[0])
        return out_tok, out_down[None]

    return jax.shard_map(
        body,
        mesh=mesh,
        in_specs=(
            P(("dp", "expert"), None),
            P(("dp", "expert"), None),
            P(("dp", "expert"), None),
            P(("dp", "expert"), None),
            P("expert", None, None),
            P("expert", None, None),
            P("expert", None, None),
        ),
        out_specs=(P(("dp", "expert"), None), P("expert", "dp", None)),
        check_vma=False,
    )
```

```python
import functools

import jax
import jax.numpy as jnp
from jax import lax
from jax.experimental import pallas as pl
from jax.experimental.pallas import tpu as pltpu
from jax.sharding import PartitionSpec as P

MESH = pl.DeviceIdType.MESH
F32, BF16 = jnp.float32, jnp.bfloat16
NT = (((1,), (1,)), ((), ()))
OFFSETS = (
    (2, 1, 0), (2, 1, 1), (3, 1, 0), (2, 0, 0), (1, 1, 0), (2, 0, 1), (1, 1, 1), (3, 1, 1),
    (1, 0, 0), (3, 0, 0), (0, 1, 0), (1, 0, 1), (3, 0, 1), (0, 1, 1), (0, 0, 1),
)


def nn(a, b):
    return jnp.dot(a, b, preferred_element_type=F32)


def nt(a, b):
    return lax.dot_general(a, b, NT, preferred_element_type=F32)


def kernel(
    nz, nx,
    tok_hbm, cot_hbm, ids, gates, wg_hbm, wu_hbm, wd_hbm,
    out_tok, out_down,
    tok, cot, wg, wu, wd, xs, xr, sd, sr, rd, rr, sel, selt, perm, hid, hidt, act, mix, hb, gb, ub,
    part, psend, precv, rsend, rrecv, fsend, frecv, fin, ybuf,
    wsem, lsem, ssem, rsem, psem, prsem, gsem, grsem, fsem, frsem, ysem,
):
    toks, width = tok.shape
    half = width // 2
    lanes = 128
    cols = half // lanes
    experts = nx * 4
    main, more = 16 * experts, 2 * experts
    rows = main + more
    hidden = wg.shape[1]
    dp, me = lax.axis_index("dp"), lax.axis_index("expert")
    yl, z = dp // nz, dp % nz
    x, yh, c = me // 4, (me // 2) % 2, me % 2

    def at(z2, y2=None):
        return ((yl if y2 is None else y2) * nz + z2 % nz, me)

    peers = []
    for dx, dy, dc in OFFSETS:
        if dx < nx:
            x2, yh2, c2, yl2 = (x + dx) % nx, (yh + dy) % 2, (c + dc) % 2, (yl + dy) % 2
            e2 = x2 * 4 + yh2 * 2 + c2
            peers.append(((yl2 * nz + z, e2), e2))
    odd = z % 2
    pairs = ((z + 1 - 2 * odd), (z + nz - 1 + 2 * odd) % nz)
    up, down = at(z + 2), at(z + nz - 2)
    across = ((1 - yl) * nz + z, me)

    barrier = pltpu.get_barrier_semaphore()
    greet = [p[0] for p in peers] + [at(p) for p in pairs] + [up, down, across]
    greet += [at(z + 2, 1 - yl), at(z + nz - 2, 1 - yl)]
    for d in greet:
        pl.semaphore_signal(barrier, inc=1, device_id=d, device_id_type=MESH)

    loads = [
        pltpu.make_async_copy(a, b, wsem.at[i])
        for i, (a, b) in enumerate(
            ((tok_hbm, tok), (cot_hbm, cot), (wg_hbm, wg), (wu_hbm, wu), (wd_hbm, wd))
        )
    ]
    for load in loads:
        load.start()

    def iota(shape, dim):
        return lax.broadcasted_iota(jnp.int32, shape, dim)

    eye = iota((toks, toks), 0) == iota((toks, toks), 1)
    before = (iota((toks, toks), 0) < iota((toks, toks), 1)).astype(F32).astype(BF16)
    idv = ids[...].astype(F32)
    gtv = gates[...].astype(F32)

    id_rows = [idv[k : k + 1] for k in (0, 1)]
    gate_rows = [gtv[k : k + 1] for k in (0, 1)]
    named = [(iota((experts, toks), 0).astype(F32) == r).astype(F32) for r in id_rows]
    earlier = nn((named[0] + named[1]).astype(BF16), before)
    slot = iota((rows, toks), 0).astype(F32)
    picks = []
    for k in (0, 1):
        pos = jnp.sum(named[k] * earlier, axis=0, keepdims=True)
        target = jnp.where(pos < 16.0, id_rows[k] * 16.0 + pos, main + id_rows[k] * 2.0 + (pos - 16.0))
        picks.append((slot == target).astype(F32))
    sel[...] = (picks[0] + picks[1]).astype(BF16)
    slot_gates = jnp.sum(picks[0] * gate_rows[0] + picks[1] * gate_rows[1], axis=1, keepdims=True)
    r0, r1 = iota((main, main), 0), iota((main, main), 1)
    perm[...] = (r1 == (r0 % cols) * more + r0 // cols).astype(F32).astype(BF16)

    def pack(buf, h):
        tall = jnp.concatenate(
            [buf[h, main:rows, j * lanes : (j + 1) * lanes] for j in range(cols)], axis=0
        )
        buf[h, 0:main, half : half + lanes] = nn(perm[...], tall).astype(BF16)

    def unpack(buf, h):
        tall = lax.dot_general(
            perm[...], buf[h, 0:main, half : half + lanes], (((0,), (0,)), ((), ())),
            preferred_element_type=F32,
        ).astype(BF16)
        for j in range(cols):
            buf[h, main:rows, j * lanes : (j + 1) * lanes] = tall[j * more : (j + 1) * more]

    def gather(src, buf, h, scale):
        def tile(t, carry):
            lo = pl.multiple_of(t * 256, 256)
            v = nn(sel[...], src[:, pl.ds(pl.multiple_of(h * half + lo, 256), 256)])
            if scale is not None:
                v = v * scale
            buf[h, 0:rows, pl.ds(lo, 256)] = v.astype(BF16)
            return carry

        lax.fori_loop(0, half // 256, tile, 0)
        pack(buf, h)

    def swap(unit, src, dst, h):
        mine = pl.ds(pl.multiple_of(me * 16, 16), 16)
        copies = [
            pltpu.make_async_remote_copy(
                src_ref=src.at[h, pl.ds(pl.multiple_of(e2 * 16, 16), 16)],
                dst_ref=dst.at[h, mine],
                send_sem=ssem.at[unit, i], recv_sem=rsem.at[unit, i],
                device_id=dev, device_id_type=MESH,
            )
            for i, (dev, e2) in enumerate(peers)
        ]
        own = pltpu.make_async_copy(src.at[h, mine], dst.at[h, mine], lsem.at[unit])
        return copies, own

    swaps = [
        swap(0, xs, xr, 0), swap(1, xs, xr, 1), swap(2, sd, sr, 0), swap(3, sd, sr, 1),
        swap(4, rd, rr, 0), swap(5, rd, rr, 1),
    ]

    def send(unit):
        copies, own = swaps[unit]
        for copy in copies:
            copy.start()
        own.start()

    def arrive(unit):
        copies, own = swaps[unit]
        for copy in copies:
            copy.wait_recv()
        own.wait()

    loads[0].wait()
    gather(tok, xs, 0, None)
    pl.semaphore_wait(barrier, len(greet))
    send(0)
    gather(tok, xs, 1, None)
    send(1)
    loads[1].wait()
    gather(cot, sd, 0, slot_gates)
    send(2)
    gather(cot, sd, 1, slot_gates)
    send(3)

    selt[...] = nt(eye.astype(F32).astype(BF16), sel[...]).astype(BF16)
    loads[2].wait()
    loads[3].wait()
    arrive(0)
    arrive(1)
    unpack(xr, 0)
    unpack(xr, 1)

    tile_f = min(256, hidden)

    def first(t, carry):
        f = pl.ds(pl.multiple_of(t * tile_f, tile_f), tile_f)
        gate = nn(xr[0, 0:rows, 0:half], wg[0:half, f]) + nn(xr[1, 0:rows, 0:half], wg[half:width, f])
        upv = nn(xr[0, 0:rows, 0:half], wu[0:half, f]) + nn(xr[1, 0:rows, 0:half], wu[half:width, f])
        s = jax.nn.sigmoid(gate)
        a = gate * s
        hid[:, f] = (a * upv).astype(BF16)
        act[:, f] = a
        mix[:, f] = upv * s * (1.0 + gate * (1.0 - s))
        return carry

    lax.fori_loop(0, hidden // tile_f, first, 0)

    def turn(t, carry):
        lo = pl.multiple_of(t * tile_f, tile_f)
        to = lo + iota((tile_f, hidden), 0)
        par, rest = to // (hidden // 2), to % (hidden // 2)
        zz, low = (rest // 16) * 2 + par, rest % 16
        source = ((low // 8) * nz + zz) * 8 + low % 8
        move = (iota((tile_f, hidden), 1) == source).astype(F32).astype(BF16)
        hidt[pl.ds(lo, tile_f), :] = nt(move, hid[...]).astype(BF16)
        return carry

    lax.fori_loop(0, hidden // tile_f, turn, 0)
    loads[4].wait()

    nodes = nz // 2
    a_mine = z // 2
    steps_up, steps_down = nodes // 2, nodes // 2 - 1

    def chunk(par, a):
        return pl.ds(pl.multiple_of(par * (hidden // 2) + (a % nodes) * 16, 16), 16)

    def order(a):
        found = []
        for k in range(steps_up):
            found.append((a + nodes // 2 - k, "up", k))
            if k < steps_down:
                found.append((a + nodes - steps_down + k, "down", k))
        return found + [(a, "own", 0)]

    def pair_copies(h):
        partner = pairs[h]
        copies = []
        for j, (a, _, _) in enumerate(order(partner // 2)):
            slot_j = pl.ds(j * 16, 16)
            copies.append(
                pltpu.make_async_remote_copy(
                    src_ref=psend.at[h, slot_j], dst_ref=precv.at[h, slot_j],
                    send_sem=psem.at[h, j], recv_sem=prsem.at[h, j],
                    device_id=at(partner), device_id_type=MESH,
                )
            )
        return copies

    pair = [pair_copies(0), pair_copies(1)]
    mine = {(way, k): (j, a) for j, (a, way, k) in enumerate(order(a_mine))}

    def products(h):
        def tile(t, carry):
            lo = pl.ds(pl.multiple_of(t * 256, 256), 256)
            part[h, :, lo] = nn(hidt[...], sr[h, 0:rows, lo])
            return carry

        lax.fori_loop(0, half // 256, tile, 0)
        for j, (a, _, _) in enumerate(order(pairs[h] // 2)):
            psend[h, j * 16 : (j + 1) * 16] = part[h, chunk(1 - odd, a), :].astype(BF16)
            pair[h][j].start()

    def backward(h):
        def back(t, carry):
            f = pl.ds(pl.multiple_of(t * tile_f, tile_f), tile_f)
            v = nt(sr[h, 0:rows, 0:half], wd[f, h * half : (h + 1) * half])
            hb[:, f] = v if h == 0 else hb[:, f] + v
            return carry

        lax.fori_loop(0, hidden // tile_f, back, 0)

    def ring_copy(h, way, k):
        d = 0 if way == "up" else 1
        span = pl.ds(k * 16, 16)
        return pltpu.make_async_remote_copy(
            src_ref=rsend.at[d, h, span], dst_ref=rrecv.at[d, h, span],
            send_sem=gsem.at[d, h, k], recv_sem=grsem.at[d, h, k],
            device_id=up if way == "up" else down, device_id_type=MESH,
        )

    def own_sum(h, way, k):
        j, a = mine[way, k]
        pair[h][j].wait_recv()
        return part[h, chunk(odd, a), :] + precv[h, j * 16 : (j + 1) * 16].astype(F32)

    ways = (("up", steps_up), ("down", steps_down))

    def final_copy(h, d, piece):
        to = z + 2 if d == 0 else z + nz - 2
        return pltpu.make_async_remote_copy(
            src_ref=fsend.at[d, h, piece], dst_ref=frecv.at[d, h, yl],
            send_sem=fsem.at[d, h, piece], recv_sem=frsem.at[d, h, yl],
            device_id=at(to, piece), device_id_type=MESH,
        )

    def final_arrival(h, d, source):
        return pltpu.make_async_remote_copy(
            src_ref=fsend.at[d, h, source], dst_ref=frecv.at[d, h, source],
            send_sem=fsem.at[d, h, source], recv_sem=frsem.at[d, h, source],
            device_id=up, device_id_type=MESH,
        )

    def ring_step(h, k):
        for d, (way, steps) in enumerate(ways):
            if k < steps:
                v = own_sum(h, way, k)
                if k > 0:
                    ring_copy(h, way, k - 1).wait_recv()
                    v = v + rrecv[d, h, (k - 1) * 16 : k * 16].astype(F32)
                if k < steps - 1:
                    rsend[d, h, k * 16 : (k + 1) * 16] = v.astype(BF16)
                    ring_copy(h, way, k).start()
                else:
                    for piece in (0, 1):
                        top = v[piece * 8 : (piece + 1) * 8]
                        folded = jnp.concatenate([top[:, : half // 2], top[:, half // 2 :]], axis=0)
                        fsend[d, h, piece] = folded.astype(BF16)
                        final_copy(h, d, piece).start()

    def row_grads(h):
        def tile(t, carry):
            lo = pl.multiple_of(t * 256, 256)
            w = pl.ds(pl.multiple_of(h * half + lo, 256), 256)
            rd[h, 0:rows, pl.ds(lo, 256)] = (nt(gb[...], wg[w, :]) + nt(ub[...], wu[w, :])).astype(BF16)
            return carry

        lax.fori_loop(0, half // 256, tile, 0)
        pack(rd, h)

    def combine(h):
        unpack(rr, h)

        def tile(t, carry):
            lo = pl.multiple_of(t * 256, 256)
            w = pl.ds(pl.multiple_of(h * half + lo, 256), 256)
            out_tok[:, w] = nn(selt[...], rr[h, 0:rows, pl.ds(lo, 256)]).astype(BF16)
            return carry

        lax.fori_loop(0, half // 256, tile, 0)

    last = pltpu.make_async_remote_copy(
        src_ref=fin.at[pl.ds(pl.multiple_of((1 - yl) * 8, 8), 8)], dst_ref=ybuf,
        send_sem=ysem.at[0], recv_sem=ysem.at[1], device_id=across, device_id_type=MESH,
    )

    arrive(2)
    unpack(sr, 0)
    products(0)
    backward(0)
    ring_step(0, 0)
    arrive(3)
    unpack(sr, 1)
    products(1)
    ring_step(0, 1)
    backward(1)
    gb[...] = (hb[...] * mix[...]).astype(BF16)
    ub[...] = (hb[...] * act[...]).astype(BF16)
    row_grads(0)
    send(4)
    ring_step(1, 0)
    ring_step(0, 2)
    row_grads(1)
    send(5)
    for k in range(1, steps_up):
        ring_step(1, k)
        ring_step(0, k + 2)
        if k == steps_up - 4:
            for h in (0, 1):
                fin[:, h * half : (h + 1) * half] = own_sum(h, "own", 0)
            last.start()
        if k >= steps_up - 2:
            h = k - (steps_up - 2)
            arrive(4 + h)
            combine(h)

    last.wait_recv()
    kept = pl.ds(pl.multiple_of(yl * 8, 8), 8)
    for h in (0, 1):
        span = slice(h * half, (h + 1) * half)
        v = fin[kept, span] + ybuf[:, span]
        for d in (0, 1):
            for source in (0, 1):
                final_arrival(h, d, source).wait_recv()
                piece = frecv[d, h, source].astype(F32)
                v = v + jnp.concatenate([piece[0:8], piece[8:16]], axis=1)
        out_down[:, span] = v

    last.wait_send()
    for copies, _ in swaps:
        for copy in copies:
            copy.wait_send()
    for h in (0, 1):
        for copy in pair[h]:
            copy.wait_send()
        for d, (way, steps) in enumerate(ways):
            for k in range(steps - 1):
                ring_copy(h, way, k).wait_send()
            for piece in (0, 1):
                final_copy(h, d, piece).wait_send()


def solution(mesh):
    nz, experts = mesh.shape["dp"] // 2, mesh.shape["expert"]

    def body(tokens, cotangent, expert_ids, gate_values, gate_weights, up_weights, down_weights):
        toks, width = tokens.shape
        hidden = gate_weights.shape[2]
        half, rows, main = width // 2, 18 * experts, 16 * experts
        n = experts - 1
        nodes = nz // 2
        vmem = pl.BlockSpec(memory_space=pltpu.VMEM)
        hbm = pl.BlockSpec(memory_space=pl.ANY)
        block = pltpu.VMEM((2, rows, half + 128), BF16)
        dma = pltpu.SemaphoreType.DMA
        flops = 2 * rows * width * hidden * 6
        out_tok, out_down = pl.pallas_call(
            functools.partial(kernel, nz, experts // 4),
            out_shape=(
                jax.ShapeDtypeStruct((toks, width), BF16),
                jax.ShapeDtypeStruct((8, width), F32),
            ),
            in_specs=[hbm] * 2 + [vmem] * 2 + [hbm] * 3,
            out_specs=(vmem, vmem),
            scratch_shapes=[
                pltpu.VMEM((toks, width), BF16), pltpu.VMEM((toks, width), BF16),
                pltpu.VMEM((width, hidden), BF16), pltpu.VMEM((width, hidden), BF16), pltpu.VMEM((hidden, width), BF16),
                block, block, block, block, block, block,
                pltpu.VMEM((rows, toks), BF16), pltpu.VMEM((toks, rows), BF16), pltpu.VMEM((main, main), BF16),
                pltpu.VMEM((rows, hidden), BF16), pltpu.VMEM((hidden, rows), BF16),
                pltpu.VMEM((rows, hidden), F32), pltpu.VMEM((rows, hidden), F32), pltpu.VMEM((rows, hidden), F32),
                pltpu.VMEM((rows, hidden), BF16), pltpu.VMEM((rows, hidden), BF16),
                pltpu.VMEM((2, hidden, half), F32),
                pltpu.VMEM((2, nodes * 16, half), BF16), pltpu.VMEM((2, nodes * 16, half), BF16),
                pltpu.VMEM((2, 2, nodes // 2 * 16, half), BF16), pltpu.VMEM((2, 2, nodes // 2 * 16, half), BF16),
                pltpu.VMEM((2, 2, 2, 16, half // 2), BF16), pltpu.VMEM((2, 2, 2, 16, half // 2), BF16),
                pltpu.VMEM((16, width), F32), pltpu.VMEM((8, width), F32),
                dma((5,)), dma((6,)), dma((6, n)), dma((6, n)),
                dma((2, nodes)), dma((2, nodes)), dma((2, 2, nodes // 2)), dma((2, 2, nodes // 2)),
                dma((2, 2, 2)), dma((2, 2, 2)), dma((2,)),
            ],
            compiler_params=pltpu.CompilerParams(
                collective_id=0, has_side_effects=True, vmem_limit_bytes=60 * 2**20
            ),
            cost_estimate=pl.CostEstimate(flops=flops, bytes_accessed=8 * 2**20, transcendentals=rows * hidden),
        )(tokens, cotangent, expert_ids.T, gate_values.T, gate_weights[0], up_weights[0], down_weights[0])
        return out_tok, out_down[None]

    return jax.shard_map(
        body,
        mesh=mesh,
        in_specs=(
            P(("dp", "expert"), None),
            P(("dp", "expert"), None),
            P(("dp", "expert"), None),
            P(("dp", "expert"), None),
            P("expert", None, None),
            P("expert", None, None),
            P("expert", None, None),
        ),
        out_specs=(P(("dp", "expert"), None), P("expert", "dp", None)),
        check_vma=False,
    )
```

```python
import functools

import jax
import jax.numpy as jnp
from jax import lax
from jax.experimental import pallas as pl
from jax.experimental.pallas import tpu as pltpu
from jax.sharding import PartitionSpec as P

MESH = pl.DeviceIdType.MESH
F32, BF16 = jnp.float32, jnp.bfloat16
NT = (((1,), (1,)), ((), ()))
OFFSETS = (
    (2, 1, 0), (2, 1, 1), (3, 1, 0), (2, 0, 0), (1, 1, 0), (2, 0, 1), (1, 1, 1), (3, 1, 1),
    (1, 0, 0), (3, 0, 0), (0, 1, 0), (1, 0, 1), (3, 0, 1), (0, 1, 1), (0, 0, 1),
)


def nn(a, b):
    return jnp.dot(a, b, preferred_element_type=F32)


def nt(a, b):
    return lax.dot_general(a, b, NT, preferred_element_type=F32)


def kernel(
    nz, nx,
    tok_hbm, cot_hbm, ids, gates, wg_hbm, wu_hbm, wd_hbm,
    out_tok, out_down,
    tok, cot, wg, wu, wd, xs, xr, sd, sr, rd, rr, sel, selt, perm, hid, hidt, act, mix, hb, gb, ub,
    part, ysend, yrecv, acc, zsend, zrecv, rsend, rrecv,
    wsem, lsem, ssem, rsem, ysem, yrsem, zsem, zrsem, gsem, grsem,
):
    toks, width = tok.shape
    half = width // 2
    lanes = 128
    cols = half // lanes
    experts = nx * 4
    main, more = 16 * experts, 2 * experts
    rows = main + more
    hidden = wg.shape[1]
    dp, me = lax.axis_index("dp"), lax.axis_index("expert")
    yl, z = dp // nz, dp % nz
    x, yh, c = me // 4, (me // 2) % 2, me % 2

    def at(z2):
        return (yl * nz + z2 % nz, me)

    peers = []
    for dx, dy, dc in OFFSETS:
        if dx < nx:
            x2, yh2, c2, yl2 = (x + dx) % nx, (yh + dy) % 2, (c + dc) % 2, (yl + dy) % 2
            e2 = x2 * 4 + yh2 * 2 + c2
            peers.append(((yl2 * nz + z, e2), e2))
    partners = [[z + nz - (z + 2 * h) % 4 + ((z + 2 * h) % 4 + t) % 4 for t in (1, 2, 3)] for h in (0, 1)]
    up, down = at(z + 4), at(z + nz - 4)
    across = ((1 - yl) * nz + z, me)

    barrier = pltpu.get_barrier_semaphore()
    greet = [p[0] for p in peers] + [at(p) for row in partners for p in row] + [up, down, across]
    for d in greet:
        pl.semaphore_signal(barrier, inc=1, device_id=d, device_id_type=MESH)

    loads = [
        pltpu.make_async_copy(a, b, wsem.at[i])
        for i, (a, b) in enumerate(
            ((tok_hbm, tok), (cot_hbm, cot), (wg_hbm, wg), (wu_hbm, wu), (wd_hbm, wd))
        )
    ]
    loads[0].start()
    loads[1].start()

    def iota(shape, dim):
        return lax.broadcasted_iota(jnp.int32, shape, dim)

    eye = iota((toks, toks), 0) == iota((toks, toks), 1)
    before = (iota((toks, toks), 0) < iota((toks, toks), 1)).astype(F32).astype(BF16)
    idv = ids[...].astype(F32)
    gtv = gates[...].astype(F32)

    id_rows = [idv[k : k + 1] for k in (0, 1)]
    gate_rows = [gtv[k : k + 1] for k in (0, 1)]
    named = [(iota((experts, toks), 0).astype(F32) == r).astype(F32) for r in id_rows]
    earlier = nn((named[0] + named[1]).astype(BF16), before)
    slot = iota((rows, toks), 0).astype(F32)
    picks = []
    for k in (0, 1):
        pos = jnp.sum(named[k] * earlier, axis=0, keepdims=True)
        target = jnp.where(pos < 16.0, id_rows[k] * 16.0 + pos, main + id_rows[k] * 2.0 + (pos - 16.0))
        picks.append((slot == target).astype(F32))
    sel[...] = (picks[0] + picks[1]).astype(BF16)
    r0, r1 = iota((main, main), 0), iota((main, main), 1)
    perm[...] = (r1 == (r0 % cols) * more + r0 // cols).astype(F32).astype(BF16)

    def pack(buf, h):
        tall = jnp.concatenate(
            [buf[h, main:rows, j * lanes : (j + 1) * lanes] for j in range(cols)], axis=0
        )
        buf[h, 0:main, half : half + lanes] = nn(perm[...], tall).astype(BF16)

    def unpack(buf, h):
        tall = lax.dot_general(
            perm[...], buf[h, 0:main, half : half + lanes], (((0,), (0,)), ((), ())),
            preferred_element_type=F32,
        ).astype(BF16)
        for j in range(cols):
            buf[h, main:rows, j * lanes : (j + 1) * lanes] = tall[j * more : (j + 1) * more]

    def gather(src, buf, h, scale):
        def tile(t, carry):
            lo = pl.multiple_of(t * 256, 256)
            v = nn(sel[...], src[:, pl.ds(pl.multiple_of(h * half + lo, 256), 256)])
            if scale is not None:
                v = v * scale
            buf[h, 0:rows, pl.ds(lo, 256)] = v.astype(BF16)
            return carry

        lax.fori_loop(0, half // 256, tile, 0, unroll=True)
        pack(buf, h)

    def swap(unit, src, dst, h):
        mine = pl.ds(pl.multiple_of(me * 16, 16), 16)
        copies = [
            pltpu.make_async_remote_copy(
                src_ref=src.at[h, pl.ds(pl.multiple_of(e2 * 16, 16), 16)],
                dst_ref=dst.at[h, mine],
                send_sem=ssem.at[unit, i], recv_sem=rsem.at[unit, i],
                device_id=dev, device_id_type=MESH,
            )
            for i, (dev, e2) in enumerate(peers)
        ]
        own = pltpu.make_async_copy(src.at[h, mine], dst.at[h, mine], lsem.at[unit])
        return copies, own

    swaps = [
        swap(0, xs, xr, 0), swap(1, xs, xr, 1), swap(2, sd, sr, 0), swap(3, sd, sr, 1),
        swap(4, rd, rr, 0), swap(5, rd, rr, 1),
    ]

    def send(unit):
        copies, own = swaps[unit]
        for copy in copies:
            copy.start()
        own.start()

    def arrive(unit):
        copies, own = swaps[unit]
        for copy in copies:
            copy.wait_recv()
        own.wait()

    loads[0].wait()
    gather(tok, xs, 0, None)
    pl.semaphore_wait(barrier, len(greet))
    send(0)
    gather(tok, xs, 1, None)
    send(1)
    for load in loads[2:]:
        load.start()
    slot_gates = jnp.sum(picks[0] * gate_rows[0] + picks[1] * gate_rows[1], axis=1, keepdims=True)
    loads[1].wait()
    gather(cot, sd, 0, slot_gates)
    send(2)
    gather(cot, sd, 1, slot_gates)
    send(3)

    selt[...] = nt(eye.astype(F32).astype(BF16), sel[...]).astype(BF16)
    loads[2].wait()
    loads[3].wait()
    arrive(0)
    arrive(1)
    unpack(xr, 0)
    unpack(xr, 1)

    tile_f = min(256, hidden)

    def first(t, carry):
        f = pl.ds(pl.multiple_of(t * tile_f, tile_f), tile_f)
        gate = nn(xr[0, 0:rows, 0:half], wg[0:half, f]) + nn(xr[1, 0:rows, 0:half], wg[half:width, f])
        upv = nn(xr[0, 0:rows, 0:half], wu[0:half, f]) + nn(xr[1, 0:rows, 0:half], wu[half:width, f])
        s = jax.nn.sigmoid(gate)
        a = gate * s
        hid[:, f] = (a * upv).astype(BF16)
        act[:, f] = a
        mix[:, f] = upv * s * (1.0 + gate * (1.0 - s))
        return carry

    lax.fori_loop(0, hidden // tile_f, first, 0)

    def turn(t, carry):
        lo = pl.multiple_of(t * tile_f, tile_f)
        move = (iota((tile_f, hidden), 1) == lo + iota((tile_f, hidden), 0)).astype(F32).astype(BF16)
        hidt[pl.ds(lo, tile_f), :] = nt(move, hid[...]).astype(BF16)
        return carry

    lax.fori_loop(0, hidden // tile_f, turn, 0)
    loads[4].wait()

    nodes = nz // 4
    node, place = z // 4, z % 4
    steps_up, steps_down = nodes // 2, nodes // 2 - 1
    order = []
    for k in range(steps_up):
        order.append((node + nodes // 2 - k) % nodes)
        if k < steps_down:
            order.append((node + nodes - steps_down + k) % nodes)
    order.append(node)
    quarter = half // 2

    def fold(v):
        return jnp.concatenate([v[:, :quarter], v[:, quarter:]], axis=0)

    def y_copy(h, j):
        span = pl.ds(j * 32, 32)
        return pltpu.make_async_remote_copy(
            src_ref=ysend.at[h, span], dst_ref=yrecv.at[h, span],
            send_sem=ysem.at[h, j], recv_sem=yrsem.at[h, j], device_id=across, device_id_type=MESH,
        )

    def z_copy(h, t, j):
        a = order[j]
        return pltpu.make_async_remote_copy(
            src_ref=zsend.at[h, t, pl.ds(j * 16, 16)],
            dst_ref=zrecv.at[h, t, pl.ds(pl.multiple_of(a * 16, 16), 16)],
            send_sem=zsem.at[h, t, j], recv_sem=zrsem.at[h, t, a],
            device_id=at(partners[h][t]), device_id_type=MESH,
        )

    def ring_copy(h, d, k):
        span = pl.ds(k * 16, 16)
        return pltpu.make_async_remote_copy(
            src_ref=rsend.at[d, h, span], dst_ref=rrecv.at[d, h, span],
            send_sem=gsem.at[d, h, k], recv_sem=grsem.at[d, h, k],
            device_id=(up, down)[d], device_id_type=MESH,
        )

    def group(y2, j):
        return pl.ds(pl.multiple_of(y2 * (hidden // 2) + order[j] * 32, 32), 32)

    def products(h):
        def tile(t, carry):
            lo = pl.ds(pl.multiple_of(t * 256, 256), 256)
            part[h, :, lo] = nn(hidt[...], sr[h, 0:rows, lo])
            return carry

        lax.fori_loop(0, half // 256, tile, 0)
        for j in range(nodes):
            ysend[h, j * 32 : (j + 1) * 32] = part[h, group(1 - yl, j), :].astype(BF16)
            y_copy(h, j).start()

    def run_of_four(h, j):
        y_copy(h, j).wait_recv()
        acc[h, j * 32 : (j + 1) * 32] = part[h, group(yl, j), :] + yrecv[h, j * 32 : (j + 1) * 32].astype(F32)
        for t in range(3):
            rows_of = pl.ds(pl.multiple_of(j * 32 + partners[h][t] % 4 * 8, 8), 8)
            zsend[h, t, j * 16 : (j + 1) * 16] = fold(acc[h, rows_of, :]).astype(BF16)
            z_copy(h, t, j).start()

    def sum_of_four(h, j):
        v = fold(acc[h, pl.ds(pl.multiple_of(j * 32 + place * 8, 8), 8), :])
        for t in range(3):
            z_copy(h, t, j).wait_recv()
            v = v + zrecv[h, t, pl.ds(pl.multiple_of(order[j] * 16, 16), 16), :].astype(F32)
        return v

    def ring_step(h, k):
        for d, steps in enumerate((steps_up, steps_down)):
            if k < steps:
                v = sum_of_four(h, 2 * k + d)
                if k > 0:
                    ring_copy(h, d, k - 1).wait_recv()
                    v = v + rrecv[d, h, (k - 1) * 16 : k * 16].astype(F32)
                rsend[d, h, k * 16 : (k + 1) * 16] = v.astype(BF16)
                ring_copy(h, d, k).start()

    def ring_end(h):
        v = sum_of_four(h, nodes - 1)
        for d, steps in enumerate((steps_up, steps_down)):
            ring_copy(h, d, steps - 1).wait_recv()
            v = v + rrecv[d, h, (steps - 1) * 16 : steps * 16].astype(F32)
        out_down[:, h * half : (h + 1) * half] = jnp.concatenate([v[0:8], v[8:16]], axis=1)

    def backward(h):
        def back(t, carry):
            f = pl.ds(pl.multiple_of(t * tile_f, tile_f), tile_f)
            v = nt(sr[h, 0:rows, 0:half], wd[f, h * half : (h + 1) * half])
            hb[:, f] = v if h == 0 else hb[:, f] + v
            return carry

        lax.fori_loop(0, hidden // tile_f, back, 0)

    def row_grads(h):
        def tile(t, carry):
            lo = pl.multiple_of(t * 256, 256)
            w = pl.ds(pl.multiple_of(h * half + lo, 256), 256)
            rd[h, 0:rows, pl.ds(lo, 256)] = (nt(gb[...], wg[w, :]) + nt(ub[...], wu[w, :])).astype(BF16)
            return carry

        lax.fori_loop(0, half // 256, tile, 0)
        pack(rd, h)

    def combine(h):
        unpack(rr, h)

        def tile(t, carry):
            lo = pl.multiple_of(t * 256, 256)
            w = pl.ds(pl.multiple_of(h * half + lo, 256), 256)
            out_tok[:, w] = nn(selt[...], rr[h, 0:rows, pl.ds(lo, 256)]).astype(BF16)
            return carry

        lax.fori_loop(0, half // 256, tile, 0)

    arrive(2)
    unpack(sr, 0)
    products(0)
    backward(0)
    run_of_four(0, 0)
    run_of_four(0, 1)
    arrive(3)
    unpack(sr, 1)
    products(1)
    run_of_four(0, 2)
    run_of_four(0, 3)
    ring_step(0, 0)
    backward(1)
    gb[...] = (hb[...] * mix[...]).astype(BF16)
    ub[...] = (hb[...] * act[...]).astype(BF16)
    row_grads(0)
    send(4)
    run_of_four(0, 4)
    run_of_four(0, 5)
    run_of_four(1, 0)
    run_of_four(1, 1)
    ring_step(0, 1)
    run_of_four(1, 2)
    run_of_four(1, 3)
    row_grads(1)
    send(5)
    ring_step(1, 0)
    run_of_four(0, 6)
    run_of_four(0, 7)
    ring_step(0, 2)
    run_of_four(1, 4)
    run_of_four(1, 5)
    ring_step(1, 1)
    ring_step(0, 3)
    run_of_four(1, 6)
    run_of_four(1, 7)
    ring_step(1, 2)
    arrive(4)
    combine(0)
    ring_step(1, 3)
    ring_end(0)
    arrive(5)
    combine(1)
    ring_end(1)

    for copies, _ in swaps:
        for copy in copies:
            copy.wait_send()
    for h in (0, 1):
        for j in range(nodes):
            y_copy(h, j).wait_send()
            for t in range(3):
                z_copy(h, t, j).wait_send()
        for d, steps in enumerate((steps_up, steps_down)):
            for k in range(steps):
                ring_copy(h, d, k).wait_send()


def solution(mesh):
    nz, experts = mesh.shape["dp"] // 2, mesh.shape["expert"]

    def body(tokens, cotangent, expert_ids, gate_values, gate_weights, up_weights, down_weights):
        toks, width = tokens.shape
        hidden = gate_weights.shape[2]
        half, rows, main = width // 2, 18 * experts, 16 * experts
        n = experts - 1
        nodes = nz // 4
        vmem = pl.BlockSpec(memory_space=pltpu.VMEM)
        hbm = pl.BlockSpec(memory_space=pl.ANY)
        block = pltpu.VMEM((2, rows, half + 128), BF16)
        dma = pltpu.SemaphoreType.DMA
        flops = 2 * rows * width * hidden * 6
        out_tok, out_down = pl.pallas_call(
            functools.partial(kernel, nz, experts // 4),
            out_shape=(
                pltpu.VMEM((toks, width), BF16),
                pltpu.VMEM((8, width), F32),
            ),
            in_specs=[hbm] * 2 + [vmem] * 2 + [hbm] * 3,
            out_specs=(vmem, vmem),
            scratch_shapes=[
                pltpu.VMEM((toks, width), BF16), pltpu.VMEM((toks, width), BF16),
                pltpu.VMEM((width, hidden), BF16), pltpu.VMEM((width, hidden), BF16), pltpu.VMEM((hidden, width), BF16),
                block, block, block, block, block, block,
                pltpu.VMEM((rows, toks), BF16), pltpu.VMEM((toks, rows), BF16), pltpu.VMEM((main, main), BF16),
                pltpu.VMEM((rows, hidden), BF16), pltpu.VMEM((hidden, rows), BF16),
                pltpu.VMEM((rows, hidden), F32), pltpu.VMEM((rows, hidden), F32), pltpu.VMEM((rows, hidden), F32),
                pltpu.VMEM((rows, hidden), BF16), pltpu.VMEM((rows, hidden), BF16),
                pltpu.VMEM((2, hidden, half), F32),
                pltpu.VMEM((2, nodes * 32, half), BF16), pltpu.VMEM((2, nodes * 32, half), BF16),
                pltpu.VMEM((2, nodes * 32, half), F32),
                pltpu.VMEM((2, 3, nodes * 16, half // 2), BF16), pltpu.VMEM((2, 3, nodes * 16, half // 2), BF16),
                pltpu.VMEM((2, 2, nodes // 2 * 16, half // 2), BF16), pltpu.VMEM((2, 2, nodes // 2 * 16, half // 2), BF16),
                dma((5,)), dma((6,)), dma((6, n)), dma((6, n)),
                dma((2, nodes)), dma((2, nodes)), dma((2, 3, nodes)), dma((2, 3, nodes)),
                dma((2, 2, nodes // 2)), dma((2, 2, nodes // 2)),
            ],
            compiler_params=pltpu.CompilerParams(
                collective_id=0, has_side_effects=True, vmem_limit_bytes=60 * 2**20
            ),
            cost_estimate=pl.CostEstimate(flops=flops, bytes_accessed=8 * 2**20, transcendentals=rows * hidden),
        )(tokens, cotangent, expert_ids.T, gate_values.T, gate_weights[0], up_weights[0], down_weights[0])
        return out_tok, out_down[None]

    return jax.shard_map(
        body,
        mesh=mesh,
        in_specs=(
            P(("dp", "expert"), None),
            P(("dp", "expert"), None),
            P(("dp", "expert"), None),
            P(("dp", "expert"), None),
            P("expert", None, None),
            P("expert", None, None),
            P("expert", None, None),
        ),
        out_specs=(P(("dp", "expert"), None), P("expert", "dp", None)),
        check_vma=False,
    )
```

```python
import functools

import jax
import jax.numpy as jnp
from jax import lax
from jax.experimental import pallas as pl
from jax.experimental.pallas import tpu as pltpu
from jax.sharding import PartitionSpec as P

MESH = pl.DeviceIdType.MESH
F32, BF16 = jnp.float32, jnp.bfloat16
NT = (((1,), (1,)), ((), ()))
OFFSETS = (
    (2, 1, 0), (2, 1, 1), (3, 1, 0), (2, 0, 0), (1, 1, 0), (2, 0, 1), (1, 1, 1), (3, 1, 1),
    (1, 0, 0), (3, 0, 0), (0, 1, 0), (1, 0, 1), (3, 0, 1), (0, 1, 1), (0, 0, 1),
)


def nn(a, b):
    return jnp.dot(a, b, preferred_element_type=F32)


def nt(a, b):
    return lax.dot_general(a, b, NT, preferred_element_type=F32)


def kernel(
    nz, nx,
    tok_hbm, cot_hbm, ids, gates, wg_hbm, wu_hbm, wd_hbm,
    out_tok, out_down,
    tok, cot, wg, wu, wd, xs, xr, sd, sr, rd, rr, sel, selt, perm, hid, hidt, act, mix, hb, gb, ub,
    part, ysend, yrecv, acc, zsend, zrecv, rsend, rrecv,
    wsem, lsem, ssem, rsem, ysem, yrsem, zsem, zrsem, gsem, grsem,
):
    toks, width = tok.shape
    half = width // 2
    lanes = 128
    cols = half // lanes
    experts = nx * 4
    main, more = 16 * experts, 2 * experts
    rows = main + more
    hidden = wg.shape[1]
    dp, me = lax.axis_index("dp"), lax.axis_index("expert")
    yl, z = dp // nz, dp % nz
    x, yh, c = me // 4, (me // 2) % 2, me % 2

    def at(z2):
        return (yl * nz + z2 % nz, me)

    peers = []
    for dx, dy, dc in OFFSETS:
        if dx < nx:
            x2, yh2, c2, yl2 = (x + dx) % nx, (yh + dy) % 2, (c + dc) % 2, (yl + dy) % 2
            e2 = x2 * 4 + yh2 * 2 + c2
            peers.append(((yl2 * nz + z, e2), e2))
    places = [(z + 2 * h) % 4 for h in (0, 1)]
    partners = [[z + nz - p + (p + t) % 4 for t in (1, 2, 3)] for p in places]
    up, down = at(z + 4), at(z + nz - 4)
    across = ((1 - yl) * nz + z, me)

    barrier = pltpu.get_barrier_semaphore()
    greet = [p[0] for p in peers] + [at(p) for row in partners for p in row] + [up, down, across]
    for d in greet:
        pl.semaphore_signal(barrier, inc=1, device_id=d, device_id_type=MESH)

    loads = [
        pltpu.make_async_copy(a, b, wsem.at[i])
        for i, (a, b) in enumerate(
            ((tok_hbm, tok), (cot_hbm, cot), (wg_hbm, wg), (wu_hbm, wu), (wd_hbm, wd))
        )
    ]
    loads[0].start()
    loads[1].start()

    def iota(shape, dim):
        return lax.broadcasted_iota(jnp.int32, shape, dim)

    eye = iota((toks, toks), 0) == iota((toks, toks), 1)
    before = (iota((toks, toks), 0) < iota((toks, toks), 1)).astype(F32).astype(BF16)
    idv = ids[...].astype(F32)
    gtv = gates[...].astype(F32)

    id_rows = [idv[k : k + 1] for k in (0, 1)]
    gate_rows = [gtv[k : k + 1] for k in (0, 1)]
    named = [(iota((experts, toks), 0).astype(F32) == r).astype(F32) for r in id_rows]
    earlier = nn((named[0] + named[1]).astype(BF16), before)
    slot = iota((rows, toks), 0).astype(F32)
    picks = []
    for k in (0, 1):
        pos = jnp.sum(named[k] * earlier, axis=0, keepdims=True)
        target = jnp.where(pos < 16.0, id_rows[k] * 16.0 + pos, main + id_rows[k] * 2.0 + (pos - 16.0))
        picks.append((slot == target).astype(F32))
    sel[...] = (picks[0] + picks[1]).astype(BF16)
    r0, r1 = iota((main, main), 0), iota((main, main), 1)
    perm[...] = (r1 == (r0 % cols) * more + r0 // cols).astype(F32).astype(BF16)

    def pack(buf, h):
        tall = jnp.concatenate(
            [buf[h, main:rows, j * lanes : (j + 1) * lanes] for j in range(cols)], axis=0
        )
        buf[h, 0:main, half : half + lanes] = nn(perm[...], tall).astype(BF16)

    def unpack(buf, h):
        tall = lax.dot_general(
            perm[...], buf[h, 0:main, half : half + lanes], (((0,), (0,)), ((), ())),
            preferred_element_type=F32,
        ).astype(BF16)
        for j in range(cols):
            buf[h, main:rows, j * lanes : (j + 1) * lanes] = tall[j * more : (j + 1) * more]

    def gather(src, buf, h, scale):
        def tile(t, carry):
            lo = pl.multiple_of(t * 256, 256)
            v = nn(sel[...], src[:, pl.ds(pl.multiple_of(h * half + lo, 256), 256)])
            if scale is not None:
                v = v * scale
            buf[h, 0:rows, pl.ds(lo, 256)] = v.astype(BF16)
            return carry

        lax.fori_loop(0, half // 256, tile, 0, unroll=True)
        pack(buf, h)

    def swap(unit, src, dst, h):
        mine = pl.ds(pl.multiple_of(me * 16, 16), 16)
        copies = [
            pltpu.make_async_remote_copy(
                src_ref=src.at[h, pl.ds(pl.multiple_of(e2 * 16, 16), 16)],
                dst_ref=dst.at[h, mine],
                send_sem=ssem.at[unit, i], recv_sem=rsem.at[unit, i],
                device_id=dev, device_id_type=MESH,
            )
            for i, (dev, e2) in enumerate(peers)
        ]
        own = pltpu.make_async_copy(src.at[h, mine], dst.at[h, mine], lsem.at[unit])
        return copies, own

    swaps = [
        swap(0, xs, xr, 0), swap(1, xs, xr, 1), swap(2, sd, sr, 0), swap(3, sd, sr, 1),
        swap(4, rd, rr, 0), swap(5, rd, rr, 1),
    ]

    def send(unit):
        copies, own = swaps[unit]
        for copy in copies:
            copy.start()
        own.start()

    def arrive(unit):
        copies, own = swaps[unit]
        for copy in copies:
            copy.wait_recv()
        own.wait()

    loads[0].wait()
    gather(tok, xs, 0, None)
    pl.semaphore_wait(barrier, len(greet))
    send(0)
    gather(tok, xs, 1, None)
    send(1)
    for load in loads[2:]:
        load.start()
    slot_gates = jnp.sum(picks[0] * gate_rows[0] + picks[1] * gate_rows[1], axis=1, keepdims=True)
    loads[1].wait()
    gather(cot, sd, 0, slot_gates)
    send(2)
    gather(cot, sd, 1, slot_gates)
    send(3)

    selt[...] = nt(eye.astype(F32).astype(BF16), sel[...]).astype(BF16)
    loads[2].wait()
    loads[3].wait()
    arrive(0)
    arrive(1)
    unpack(xr, 0)
    unpack(xr, 1)

    tile_f = min(256, hidden)

    def first(t, carry):
        f = pl.ds(pl.multiple_of(t * tile_f, tile_f), tile_f)
        gate = nn(xr[0, 0:rows, 0:half], wg[0:half, f]) + nn(xr[1, 0:rows, 0:half], wg[half:width, f])
        upv = nn(xr[0, 0:rows, 0:half], wu[0:half, f]) + nn(xr[1, 0:rows, 0:half], wu[half:width, f])
        s = jax.nn.sigmoid(gate)
        a = gate * s
        hid[:, f] = (a * upv).astype(BF16)
        act[:, f] = a
        mix[:, f] = upv * s * (1.0 + gate * (1.0 - s))
        return carry

    lax.fori_loop(0, hidden // tile_f, first, 0)

    def turn(t, carry):
        lo = pl.multiple_of(t * tile_f, tile_f)
        move = (iota((tile_f, hidden), 1) == lo + iota((tile_f, hidden), 0)).astype(F32).astype(BF16)
        hidt[pl.ds(lo, tile_f), :] = nt(move, hid[...]).astype(BF16)
        return carry

    lax.fori_loop(0, hidden // tile_f, turn, 0)
    loads[4].wait()

    nodes = nz // 4
    steps_up, steps_down = nodes // 2, nodes // 2 - 1

    def order_of(node):
        found = []
        for k in range(steps_up):
            found.append((node + nodes // 2 - k) % nodes)
            if k < steps_down:
                found.append((node + nodes - steps_down + k) % nodes)
        return found + [node]

    orders = [order_of((z + 2 * h) % nz // 4) for h in (0, 1)]
    quarter = half // 2

    def fold(v):
        return jnp.concatenate([v[:, :quarter], v[:, quarter:]], axis=0)

    def y_copy(h, j):
        span = pl.ds(j * 32, 32)
        return pltpu.make_async_remote_copy(
            src_ref=ysend.at[h, span], dst_ref=yrecv.at[h, span],
            send_sem=ysem.at[h, j], recv_sem=yrsem.at[h, j], device_id=across, device_id_type=MESH,
        )

    def z_copy(h, t, j):
        span = pl.ds(j * 16, 16)
        return pltpu.make_async_remote_copy(
            src_ref=zsend.at[h, t, span], dst_ref=zrecv.at[h, t, span],
            send_sem=zsem.at[h, t, j], recv_sem=zrsem.at[h, t, j],
            device_id=at(partners[h][t]), device_id_type=MESH,
        )

    def ring_copy(h, d, k):
        span = pl.ds(k * 16, 16)
        return pltpu.make_async_remote_copy(
            src_ref=rsend.at[d, h, span], dst_ref=rrecv.at[d, h, span],
            send_sem=gsem.at[d, h, k], recv_sem=grsem.at[d, h, k],
            device_id=(up, down)[d], device_id_type=MESH,
        )

    def group(h, y2, j):
        found = []
        for two in (0, 2):
            row = y2 * (hidden // 2) + (orders[h][j] * 4 + nz - 2 * h + two) % nz * 8
            found.append(part[h, pl.ds(pl.multiple_of(row, 16), 16), :])
        return jnp.concatenate(found, axis=0)

    def products(h):
        def tile(t, carry):
            lo = pl.ds(pl.multiple_of(t * 256, 256), 256)
            part[h, :, lo] = nn(hidt[...], sr[h, 0:rows, lo])
            return carry

        lax.fori_loop(0, half // 256, tile, 0)

    def y_start(h, *js):
        for j in js:
            ysend[h, j * 32 : (j + 1) * 32] = group(h, 1 - yl, j).astype(BF16)
            y_copy(h, j).start()

    def run_of_four(h, *js):
        for j in js:
            y_copy(h, j).wait_recv()
            acc[h, j * 32 : (j + 1) * 32] = group(h, yl, j) + yrecv[h, j * 32 : (j + 1) * 32].astype(F32)
            for t in range(3):
                rows_of = pl.ds(pl.multiple_of(j * 32 + (places[h] + t + 1) % 4 * 8, 8), 8)
                zsend[h, t, j * 16 : (j + 1) * 16] = fold(acc[h, rows_of, :]).astype(BF16)
                z_copy(h, t, j).start()

    def sum_of_four(h, j):
        v = fold(acc[h, pl.ds(pl.multiple_of(j * 32 + places[h] * 8, 8), 8), :])
        for t in range(3):
            z_copy(h, t, j).wait_recv()
            v = v + zrecv[h, t, j * 16 : (j + 1) * 16].astype(F32)
        return v

    def ring_step(h, k):
        for d, steps in enumerate((steps_up, steps_down)):
            if k < steps:
                v = sum_of_four(h, 2 * k + d)
                if k > 0:
                    ring_copy(h, d, k - 1).wait_recv()
                    v = v + rrecv[d, h, (k - 1) * 16 : k * 16].astype(F32)
                rsend[d, h, k * 16 : (k + 1) * 16] = v.astype(BF16)
                ring_copy(h, d, k).start()

    def ring_end(h):
        v = sum_of_four(h, nodes - 1)
        for d, steps in enumerate((steps_up, steps_down)):
            ring_copy(h, d, steps - 1).wait_recv()
            v = v + rrecv[d, h, (steps - 1) * 16 : steps * 16].astype(F32)
        out_down[:, h * half : (h + 1) * half] = jnp.concatenate([v[0:8], v[8:16]], axis=1)

    def backward(h):
        def back(t, carry):
            f = pl.ds(pl.multiple_of(t * tile_f, tile_f), tile_f)
            v = nt(sr[h, 0:rows, 0:half], wd[f, h * half : (h + 1) * half])
            hb[:, f] = v if h == 0 else hb[:, f] + v
            return carry

        lax.fori_loop(0, hidden // tile_f, back, 0)

    def row_grads(h):
        def tile(t, carry):
            lo = pl.multiple_of(t * 256, 256)
            w = pl.ds(pl.multiple_of(h * half + lo, 256), 256)
            rd[h, 0:rows, pl.ds(lo, 256)] = (nt(gb[...], wg[w, :]) + nt(ub[...], wu[w, :])).astype(BF16)
            return carry

        lax.fori_loop(0, half // 256, tile, 0)
        pack(rd, h)

    def combine(h):
        unpack(rr, h)

        def tile(t, carry):
            lo = pl.multiple_of(t * 256, 256)
            w = pl.ds(pl.multiple_of(h * half + lo, 256), 256)
            out_tok[:, w] = nn(selt[...], rr[h, 0:rows, pl.ds(lo, 256)]).astype(BF16)
            return carry

        lax.fori_loop(0, half // 256, tile, 0)

    arrive(2)
    unpack(sr, 0)
    products(0)
    y_start(0, 0, 1, 2, 3)
    backward(0)
    run_of_four(0, 0, 1)
    arrive(3)
    unpack(sr, 1)
    products(1)
    y_start(1, 0, 1)
    y_start(0, 4, 5)
    y_start(1, 2, 3)
    y_start(0, 6, 7)
    y_start(1, 4, 5, 6, 7)
    run_of_four(0, 2, 3)
    backward(1)
    gb[...] = (hb[...] * mix[...]).astype(BF16)
    ub[...] = (hb[...] * act[...]).astype(BF16)
    ring_step(0, 0)
    row_grads(0)
    send(4)
    run_of_four(1, 0, 1)
    ring_step(0, 1)
    run_of_four(0, 4, 5)
    ring_step(1, 0)
    row_grads(1)
    send(5)
    run_of_four(1, 2, 3)
    ring_step(0, 2)
    run_of_four(0, 6, 7)
    ring_step(1, 1)
    run_of_four(1, 4, 5)
    ring_step(0, 3)
    run_of_four(1, 6, 7)
    ring_step(1, 2)
    arrive(4)
    combine(0)
    ring_end(0)
    ring_step(1, 3)
    arrive(5)
    combine(1)
    ring_end(1)

    for copies, _ in swaps:
        for copy in copies:
            copy.wait_send()
    for h in (0, 1):
        for j in range(nodes):
            y_copy(h, j).wait_send()
            for t in range(3):
                z_copy(h, t, j).wait_send()
        for d, steps in enumerate((steps_up, steps_down)):
            for k in range(steps):
                ring_copy(h, d, k).wait_send()


def solution(mesh):
    nz, experts = mesh.shape["dp"] // 2, mesh.shape["expert"]

    def body(tokens, cotangent, expert_ids, gate_values, gate_weights, up_weights, down_weights):
        toks, width = tokens.shape
        hidden = gate_weights.shape[2]
        half, rows, main = width // 2, 18 * experts, 16 * experts
        n = experts - 1
        nodes = nz // 4
        vmem = pl.BlockSpec(memory_space=pltpu.VMEM)
        hbm = pl.BlockSpec(memory_space=pl.ANY)
        block = pltpu.VMEM((2, rows, half + 128), BF16)
        dma = pltpu.SemaphoreType.DMA
        flops = 2 * rows * width * hidden * 6
        out_tok, out_down = pl.pallas_call(
            functools.partial(kernel, nz, experts // 4),
            out_shape=(
                pltpu.VMEM((toks, width), BF16),
                pltpu.VMEM((8, width), F32),
            ),
            in_specs=[hbm] * 2 + [vmem] * 2 + [hbm] * 3,
            out_specs=(vmem, vmem),
            scratch_shapes=[
                pltpu.VMEM((toks, width), BF16), pltpu.VMEM((toks, width), BF16),
                pltpu.VMEM((width, hidden), BF16), pltpu.VMEM((width, hidden), BF16), pltpu.VMEM((hidden, width), BF16),
                block, block, block, block, block, block,
                pltpu.VMEM((rows, toks), BF16), pltpu.VMEM((toks, rows), BF16), pltpu.VMEM((main, main), BF16),
                pltpu.VMEM((rows, hidden), BF16), pltpu.VMEM((hidden, rows), BF16),
                pltpu.VMEM((rows, hidden), F32), pltpu.VMEM((rows, hidden), F32), pltpu.VMEM((rows, hidden), F32),
                pltpu.VMEM((rows, hidden), BF16), pltpu.VMEM((rows, hidden), BF16),
                pltpu.VMEM((2, hidden, half), F32),
                pltpu.VMEM((2, nodes * 32, half), BF16), pltpu.VMEM((2, nodes * 32, half), BF16),
                pltpu.VMEM((2, nodes * 32, half), F32),
                pltpu.VMEM((2, 3, nodes * 16, half // 2), BF16), pltpu.VMEM((2, 3, nodes * 16, half // 2), BF16),
                pltpu.VMEM((2, 2, nodes // 2 * 16, half // 2), BF16), pltpu.VMEM((2, 2, nodes // 2 * 16, half // 2), BF16),
                dma((5,)), dma((6,)), dma((6, n)), dma((6, n)),
                dma((2, nodes)), dma((2, nodes)), dma((2, 3, nodes)), dma((2, 3, nodes)),
                dma((2, 2, nodes // 2)), dma((2, 2, nodes // 2)),
            ],
            compiler_params=pltpu.CompilerParams(
                collective_id=0, has_side_effects=True, vmem_limit_bytes=60 * 2**20
            ),
            cost_estimate=pl.CostEstimate(flops=flops, bytes_accessed=8 * 2**20, transcendentals=rows * hidden),
        )(tokens, cotangent, expert_ids.T, gate_values.T, gate_weights[0], up_weights[0], down_weights[0])
        return out_tok, out_down[None]

    return jax.shard_map(
        body,
        mesh=mesh,
        in_specs=(
            P(("dp", "expert"), None),
            P(("dp", "expert"), None),
            P(("dp", "expert"), None),
            P(("dp", "expert"), None),
            P("expert", None, None),
            P("expert", None, None),
            P("expert", None, None),
        ),
        out_specs=(P(("dp", "expert"), None), P("expert", "dp", None)),
        check_vma=False,
    )
```

```python
import functools

import jax
import jax.numpy as jnp
from jax import lax
from jax.experimental import pallas as pl
from jax.experimental.pallas import tpu as pltpu
from jax.sharding import PartitionSpec as P

MESH = pl.DeviceIdType.MESH
F32, BF16 = jnp.float32, jnp.bfloat16
NT = (((1,), (1,)), ((), ()))
OFFSETS = (
    (2, 1, 0), (2, 1, 1), (3, 1, 0), (2, 0, 0), (1, 1, 0), (2, 0, 1), (1, 1, 1), (3, 1, 1),
    (1, 0, 0), (3, 0, 0), (0, 1, 0), (1, 0, 1), (3, 0, 1), (0, 1, 1), (0, 0, 1),
)


def nn(a, b):
    return jnp.dot(a, b, preferred_element_type=F32)


def nt(a, b):
    return lax.dot_general(a, b, NT, preferred_element_type=F32)


def kernel(
    nz, nx,
    tok_hbm, cot_hbm, ids, gates, wg_hbm, wu_hbm, wd_hbm,
    out_tok, out_down,
    tok, cot, wg, wu, wd, xs, xr, sd, sr, rd, rr, sel, selt, perm, hid, hidt, act, mix, hb, gb, ub,
    part, ysend, yrecv, acc, zsend, zrecv, rsend, rrecv,
    wsem, lsem, ssem, rsem, ysem, yrsem, zsem, zrsem, gsem, grsem,
):
    toks, width = tok.shape
    half = width // 2
    lanes = 128
    cols = half // lanes
    experts = nx * 4
    main, more = 16 * experts, 2 * experts
    rows = main + more
    hidden = wg.shape[1]
    dp, me = lax.axis_index("dp"), lax.axis_index("expert")
    yl, z = dp // nz, dp % nz
    x, yh, c = me // 4, (me // 2) % 2, me % 2

    def at(z2):
        return (yl * nz + z2 % nz, me)

    peers = []
    for dx, dy, dc in OFFSETS:
        if dx < nx:
            x2, yh2, c2, yl2 = (x + dx) % nx, (yh + dy) % 2, (c + dc) % 2, (yl + dy) % 2
            e2 = x2 * 4 + yh2 * 2 + c2
            peers.append(((yl2 * nz + z, e2), e2))
    places = [(z + 2 * h) % 4 for h in (0, 1)]
    partners = [[z + nz - p + (p + t) % 4 for t in (1, 2, 3)] for p in places]
    up, down = at(z + 4), at(z + nz - 4)
    across = ((1 - yl) * nz + z, me)

    barrier = pltpu.get_barrier_semaphore()
    greet = [p[0] for p in peers] + [at(p) for row in partners for p in row] + [up, down, across]
    for d in greet:
        pl.semaphore_signal(barrier, inc=1, device_id=d, device_id_type=MESH)

    loads = [
        pltpu.make_async_copy(a, b, wsem.at[i])
        for i, (a, b) in enumerate(
            ((tok_hbm, tok), (cot_hbm, cot), (wg_hbm, wg), (wu_hbm, wu), (wd_hbm, wd))
        )
    ]
    loads[0].start()
    loads[1].start()

    def iota(shape, dim):
        return lax.broadcasted_iota(jnp.int32, shape, dim)

    eye = iota((toks, toks), 0) == iota((toks, toks), 1)
    before = (iota((toks, toks), 0) < iota((toks, toks), 1)).astype(F32).astype(BF16)
    idv = ids[...].astype(F32)
    gtv = gates[...].astype(F32)

    id_rows = [idv[k : k + 1] for k in (0, 1)]
    gate_rows = [gtv[k : k + 1] for k in (0, 1)]
    named = [(iota((experts, toks), 0).astype(F32) == r).astype(F32) for r in id_rows]
    earlier = nn((named[0] + named[1]).astype(BF16), before)
    slot = iota((rows, toks), 0).astype(F32)
    picks = []
    for k in (0, 1):
        pos = jnp.sum(named[k] * earlier, axis=0, keepdims=True)
        target = jnp.where(pos < 16.0, id_rows[k] * 16.0 + pos, main + id_rows[k] * 2.0 + (pos - 16.0))
        picks.append((slot == target).astype(F32))
    sel[...] = (picks[0] + picks[1]).astype(BF16)
    r0, r1 = iota((main, main), 0), iota((main, main), 1)
    perm[...] = (r1 == (r0 % cols) * more + r0 // cols).astype(F32).astype(BF16)

    def pack(buf, h):
        tall = jnp.concatenate(
            [buf[h, main:rows, j * lanes : (j + 1) * lanes] for j in range(cols)], axis=0
        )
        buf[h, 0:main, half : half + lanes] = nn(perm[...], tall).astype(BF16)

    def unpack(buf, h):
        tall = lax.dot_general(
            perm[...], buf[h, 0:main, half : half + lanes], (((0,), (0,)), ((), ())),
            preferred_element_type=F32,
        ).astype(BF16)
        for j in range(cols):
            buf[h, main:rows, j * lanes : (j + 1) * lanes] = tall[j * more : (j + 1) * more]

    def gather(src, buf, h, scale):
        def tile(t, carry):
            lo = pl.multiple_of(t * 256, 256)
            v = nn(sel[...], src[:, pl.ds(pl.multiple_of(h * half + lo, 256), 256)])
            if scale is not None:
                v = v * scale
            buf[h, 0:rows, pl.ds(lo, 256)] = v.astype(BF16)
            return carry

        lax.fori_loop(0, half // 256, tile, 0, unroll=True)
        pack(buf, h)

    def swap(unit, src, dst, h):
        mine = pl.ds(pl.multiple_of(me * 16, 16), 16)
        copies = [
            pltpu.make_async_remote_copy(
                src_ref=src.at[h, pl.ds(pl.multiple_of(e2 * 16, 16), 16)],
                dst_ref=dst.at[h, mine],
                send_sem=ssem.at[unit, i], recv_sem=rsem.at[unit, i],
                device_id=dev, device_id_type=MESH,
            )
            for i, (dev, e2) in enumerate(peers)
        ]
        own = pltpu.make_async_copy(src.at[h, mine], dst.at[h, mine], lsem.at[unit])
        return copies, own

    swaps = [
        swap(0, xs, xr, 0), swap(1, xs, xr, 1), swap(2, sd, sr, 0), swap(3, sd, sr, 1),
        swap(4, rd, rr, 0), swap(5, rd, rr, 1),
    ]

    def send(unit):
        copies, own = swaps[unit]
        for copy in copies:
            copy.start()
        own.start()

    def arrive(unit):
        copies, own = swaps[unit]
        for copy in copies:
            copy.wait_recv()
        own.wait()

    loads[0].wait()
    gather(tok, xs, 0, None)
    pl.semaphore_wait(barrier, len(greet))
    send(0)
    gather(tok, xs, 1, None)
    send(1)
    for load in loads[2:]:
        load.start()
    slot_gates = jnp.sum(picks[0] * gate_rows[0] + picks[1] * gate_rows[1], axis=1, keepdims=True)
    loads[1].wait()
    gather(cot, sd, 0, slot_gates)
    send(2)
    gather(cot, sd, 1, slot_gates)
    send(3)

    selt[...] = nt(eye.astype(F32).astype(BF16), sel[...]).astype(BF16)
    loads[2].wait()
    loads[3].wait()
    arrive(0)
    arrive(1)
    unpack(xr, 0)
    unpack(xr, 1)

    tile_f = min(256, hidden)

    def first(t, carry):
        f = pl.ds(pl.multiple_of(t * tile_f, tile_f), tile_f)
        gate = nn(xr[0, 0:rows, 0:half], wg[0:half, f]) + nn(xr[1, 0:rows, 0:half], wg[half:width, f])
        upv = nn(xr[0, 0:rows, 0:half], wu[0:half, f]) + nn(xr[1, 0:rows, 0:half], wu[half:width, f])
        s = jax.nn.sigmoid(gate)
        a = gate * s
        hid[:, f] = (a * upv).astype(BF16)
        act[:, f] = a
        mix[:, f] = upv * s * (1.0 + gate * (1.0 - s))
        return carry

    lax.fori_loop(0, hidden // tile_f, first, 0)

    def turn(t, carry):
        lo = pl.multiple_of(t * tile_f, tile_f)
        move = (iota((tile_f, hidden), 1) == lo + iota((tile_f, hidden), 0)).astype(F32).astype(BF16)
        hidt[pl.ds(lo, tile_f), :] = nt(move, hid[...]).astype(BF16)
        return carry

    lax.fori_loop(0, hidden // tile_f, turn, 0)
    loads[4].wait()

    nodes = nz // 4
    steps_up, steps_down = nodes // 2, nodes // 2 - 1

    def order_of(node):
        found = []
        for k in range(steps_up):
            found.append((node + nodes // 2 - k) % nodes)
            if k < steps_down:
                found.append((node + nodes - steps_down + k) % nodes)
        return found + [node]

    orders = [order_of((z + 2 * h) % nz // 4) for h in (0, 1)]
    quarter = half // 2

    def fold(v):
        return jnp.concatenate([v[:, :quarter], v[:, quarter:]], axis=0)

    def y_copy(h, j):
        span = pl.ds(j * 32, 32)
        return pltpu.make_async_remote_copy(
            src_ref=ysend.at[h, span], dst_ref=yrecv.at[h, span],
            send_sem=ysem.at[h, j], recv_sem=yrsem.at[h, j], device_id=across, device_id_type=MESH,
        )

    def z_copy(h, t, j):
        span = pl.ds(j * 16, 16)
        return pltpu.make_async_remote_copy(
            src_ref=zsend.at[h, t, span], dst_ref=zrecv.at[h, t, span],
            send_sem=zsem.at[h, t, j], recv_sem=zrsem.at[h, t, j],
            device_id=at(partners[h][t]), device_id_type=MESH,
        )

    def ring_copy(h, d, k):
        span = pl.ds(k * 16, 16)
        return pltpu.make_async_remote_copy(
            src_ref=rsend.at[d, h, span], dst_ref=rrecv.at[d, h, span],
            send_sem=gsem.at[d, h, k], recv_sem=grsem.at[d, h, k],
            device_id=(up, down)[d], device_id_type=MESH,
        )

    def group(h, y2, j):
        found = []
        for two in (0, 2):
            row = y2 * (hidden // 2) + (orders[h][j] * 4 + nz - 2 * h + two) % nz * 8
            found.append(part[h, pl.ds(pl.multiple_of(row, 16), 16), :])
        return jnp.concatenate(found, axis=0)

    def products(h):
        def tile(t, carry):
            lo = pl.ds(pl.multiple_of(t * 256, 256), 256)
            part[h, :, lo] = nn(hidt[...], sr[h, 0:rows, lo])
            return carry

        lax.fori_loop(0, half // 256, tile, 0, unroll=True)

    def y_start(h, *js):
        for j in js:
            ysend[h, j * 32 : (j + 1) * 32] = group(h, 1 - yl, j).astype(BF16)
            y_copy(h, j).start()

    def run_of_four(h, *js):
        for j in js:
            y_copy(h, j).wait_recv()
            acc[h, j * 32 : (j + 1) * 32] = group(h, yl, j) + yrecv[h, j * 32 : (j + 1) * 32].astype(F32)
            for t in range(3):
                rows_of = pl.ds(pl.multiple_of(j * 32 + (places[h] + t + 1) % 4 * 8, 8), 8)
                zsend[h, t, j * 16 : (j + 1) * 16] = fold(acc[h, rows_of, :]).astype(BF16)
                z_copy(h, t, j).start()

    def sum_of_four(h, j):
        v = fold(acc[h, pl.ds(pl.multiple_of(j * 32 + places[h] * 8, 8), 8), :])
        for t in range(3):
            z_copy(h, t, j).wait_recv()
            v = v + zrecv[h, t, j * 16 : (j + 1) * 16].astype(F32)
        return v

    def ring_step(h, k):
        for d, steps in enumerate((steps_up, steps_down)):
            if k < steps:
                v = sum_of_four(h, 2 * k + d)
                if k > 0:
                    ring_copy(h, d, k - 1).wait_recv()
                    v = v + rrecv[d, h, (k - 1) * 16 : k * 16].astype(F32)
                rsend[d, h, k * 16 : (k + 1) * 16] = v.astype(BF16)
                ring_copy(h, d, k).start()

    def ring_end(h):
        v = sum_of_four(h, nodes - 1)
        for d, steps in enumerate((steps_up, steps_down)):
            ring_copy(h, d, steps - 1).wait_recv()
            v = v + rrecv[d, h, (steps - 1) * 16 : steps * 16].astype(F32)
        out_down[:, h * half : (h + 1) * half] = jnp.concatenate([v[0:8], v[8:16]], axis=1)

    def backward(h):
        def back(t, carry):
            f = pl.ds(pl.multiple_of(t * tile_f, tile_f), tile_f)
            v = nt(sr[h, 0:rows, 0:half], wd[f, h * half : (h + 1) * half])
            hb[:, f] = v if h == 0 else hb[:, f] + v
            return carry

        lax.fori_loop(0, hidden // tile_f, back, 0, unroll=True)

    def row_grads(h):
        def tile(t, carry):
            lo = pl.multiple_of(t * 256, 256)
            w = pl.ds(pl.multiple_of(h * half + lo, 256), 256)
            rd[h, 0:rows, pl.ds(lo, 256)] = (nt(gb[...], wg[w, :]) + nt(ub[...], wu[w, :])).astype(BF16)
            return carry

        lax.fori_loop(0, half // 256, tile, 0, unroll=True)
        pack(rd, h)

    def combine(h):
        unpack(rr, h)

        def tile(t, carry):
            lo = pl.multiple_of(t * 256, 256)
            w = pl.ds(pl.multiple_of(h * half + lo, 256), 256)
            out_tok[:, w] = nn(selt[...], rr[h, 0:rows, pl.ds(lo, 256)]).astype(BF16)
            return carry

        lax.fori_loop(0, half // 256, tile, 0)

    arrive(2)
    unpack(sr, 0)
    products(0)
    y_start(0, 0, 1, 2, 3)
    backward(0)
    run_of_four(0, 0, 1)
    arrive(3)
    unpack(sr, 1)
    products(1)
    y_start(1, 0, 1, 2, 3)
    y_start(0, 4, 5)
    y_start(1, 4, 5)
    y_start(0, 6, 7)
    y_start(1, 6, 7)
    run_of_four(0, 2, 3)
    backward(1)
    gb[...] = (hb[...] * mix[...]).astype(BF16)
    ub[...] = (hb[...] * act[...]).astype(BF16)
    ring_step(0, 0)
    run_of_four(1, 0, 1)
    row_grads(0)
    send(4)
    run_of_four(1, 2, 3)
    ring_step(0, 1)
    ring_step(1, 0)
    row_grads(1)
    send(5)
    run_of_four(0, 4, 5)
    run_of_four(1, 4, 5)
    ring_step(1, 1)
    ring_step(0, 2)
    run_of_four(0, 6, 7)
    run_of_four(1, 6, 7)
    ring_step(1, 2)
    ring_step(0, 3)
    arrive(4)
    combine(0)
    ring_step(1, 3)
    ring_end(0)
    arrive(5)
    combine(1)
    ring_end(1)

    for copies, _ in swaps:
        for copy in copies:
            copy.wait_send()
    for h in (0, 1):
        for j in range(nodes):
            y_copy(h, j).wait_send()
            for t in range(3):
                z_copy(h, t, j).wait_send()
        for d, steps in enumerate((steps_up, steps_down)):
            for k in range(steps):
                ring_copy(h, d, k).wait_send()


def solution(mesh):
    nz, experts = mesh.shape["dp"] // 2, mesh.shape["expert"]

    def body(tokens, cotangent, expert_ids, gate_values, gate_weights, up_weights, down_weights):
        toks, width = tokens.shape
        hidden = gate_weights.shape[2]
        half, rows, main = width // 2, 18 * experts, 16 * experts
        n = experts - 1
        nodes = nz // 4
        vmem = pl.BlockSpec(memory_space=pltpu.VMEM)
        hbm = pl.BlockSpec(memory_space=pl.ANY)
        block = pltpu.VMEM((2, rows, half + 128), BF16)
        dma = pltpu.SemaphoreType.DMA
        flops = 2 * rows * width * hidden * 6
        out_tok, out_down = pl.pallas_call(
            functools.partial(kernel, nz, experts // 4),
            out_shape=(
                pltpu.VMEM((toks, width), BF16),
                pltpu.VMEM((8, width), F32),
            ),
            in_specs=[hbm] * 2 + [vmem] * 2 + [hbm] * 3,
            out_specs=(vmem, vmem),
            scratch_shapes=[
                pltpu.VMEM((toks, width), BF16), pltpu.VMEM((toks, width), BF16),
                pltpu.VMEM((width, hidden), BF16), pltpu.VMEM((width, hidden), BF16), pltpu.VMEM((hidden, width), BF16),
                block, block, block, block, block, block,
                pltpu.VMEM((rows, toks), BF16), pltpu.VMEM((toks, rows), BF16), pltpu.VMEM((main, main), BF16),
                pltpu.VMEM((rows, hidden), BF16), pltpu.VMEM((hidden, rows), BF16),
                pltpu.VMEM((rows, hidden), F32), pltpu.VMEM((rows, hidden), F32), pltpu.VMEM((rows, hidden), F32),
                pltpu.VMEM((rows, hidden), BF16), pltpu.VMEM((rows, hidden), BF16),
                pltpu.VMEM((2, hidden, half), F32),
                pltpu.VMEM((2, nodes * 32, half), BF16), pltpu.VMEM((2, nodes * 32, half), BF16),
                pltpu.VMEM((2, nodes * 32, half), F32),
                pltpu.VMEM((2, 3, nodes * 16, half // 2), BF16), pltpu.VMEM((2, 3, nodes * 16, half // 2), BF16),
                pltpu.VMEM((2, 2, nodes // 2 * 16, half // 2), BF16), pltpu.VMEM((2, 2, nodes // 2 * 16, half // 2), BF16),
                dma((5,)), dma((6,)), dma((6, n)), dma((6, n)),
                dma((2, nodes)), dma((2, nodes)), dma((2, 3, nodes)), dma((2, 3, nodes)),
                dma((2, 2, nodes // 2)), dma((2, 2, nodes // 2)),
            ],
            compiler_params=pltpu.CompilerParams(
                collective_id=0, has_side_effects=True, vmem_limit_bytes=60 * 2**20
            ),
            cost_estimate=pl.CostEstimate(flops=flops, bytes_accessed=8 * 2**20, transcendentals=rows * hidden),
        )(tokens, cotangent, expert_ids.T, gate_values.T, gate_weights[0], up_weights[0], down_weights[0])
        return out_tok, out_down[None]

    return jax.shard_map(
        body,
        mesh=mesh,
        in_specs=(
            P(("dp", "expert"), None),
            P(("dp", "expert"), None),
            P(("dp", "expert"), None),
            P(("dp", "expert"), None),
            P("expert", None, None),
            P("expert", None, None),
            P("expert", None, None),
        ),
        out_specs=(P(("dp", "expert"), None), P("expert", "dp", None)),
        check_vma=False,
    )
```
